256 devices in a mesh: plane: 16 (over z, x_lo), elem: 16 (over x_hi, y, core).
Axes of the slice: x: 4 (x_hi: 2, x_lo: 2; x = x_hi * 2 + x_lo), y: 4, z: 8, core: 2. Of those that a mesh axis runs over, the one named last changes fastest.
Arguments:
- velocity_modes: float32 [2, 3, 1024, 16384], P(None, None, 'plane', 'elem'), may hold values from -1.5 to 1.5
- geometry: float32 [4, 16384], P(None, 'elem'), may hold values from -4 to 4
- neighbour: int32 [256, 4], P('elem'), may hold values from -1 to 255, as said below
- neighbour_edge: int32 [256, 4], P('elem'), may hold values from 0 to 3, as said below
- flipped: int32 [256, 4], P('elem'), may hold values from 0 to 1
Outputs:
- advection: float32 [2, 3, 1024, 16384], P(None, None, 'plane', 'elem')
The draws below stay inside these ranges and needn't reach their ends.
Inputs may be any that keep to these rules, and one draw needn't show every extreme that they name: Element e belongs to index e // 16 of elem. Every neighbour belongs to the same index or to the one before or after it, cyclically. Neighbours are mutual: if edge k of a meets edge k2 of b, edge k2 of b meets edge k of a. `neighbour_edge`: 0 where neighbour is -1.
All inputs are finite; a program needn't handle non-finite values.
Results may differ from the reference program's by a relative error of at most 0.00015.
Values sent between devices are 32-bit elements; how exact they have to be, the bound alone decides.
A program may use at most 64 MiB of HBM per device.

```python
import jax
import jax.numpy as jnp
import numpy as np
from jax import lax

PLANES = 1024
POINTS = 64
ELEM_DEV = 16
ELEMENTS = 256
GRID_POINTS = 16384


def build_mesh(key):
    row_width = ELEM_DEV // 2
    row_count = ELEMENTS // row_width
    device_count = ELEMENTS // ELEM_DEV
    perm_keys = jax.random.split(jax.random.fold_in(key, 11), device_count)
    shuffles = jax.vmap(lambda one_key: jax.random.permutation(one_key, ELEM_DEV))(perm_keys)
    cell_ids = jnp.arange(ELEMENTS, dtype=jnp.int32)
    owner = cell_ids // ELEM_DEV
    elem_of_cell = owner * ELEM_DEV + shuffles.reshape(-1).astype(jnp.int32)
    cell_of_elem = jnp.zeros((ELEMENTS,), jnp.int32).at[elem_of_cell].set(cell_ids)
    turns = jax.random.randint(jax.random.fold_in(key, 12), (ELEMENTS,), 0, 4).astype(jnp.int32)
    cell_row = cell_of_elem // row_width
    cell_col = cell_of_elem % row_width
    edge_ids = jnp.arange(4, dtype=jnp.int32)[None, :]
    direction = (edge_ids + turns[:, None]) % 4
    row_step = jnp.where(direction == 0, -1, jnp.where(direction == 2, 1, 0))
    col_step = jnp.where(direction == 1, 1, jnp.where(direction == 3, -1, 0))
    new_row = (cell_row[:, None] + row_step) % row_count
    new_col = cell_col[:, None] + col_step
    inside = (new_col >= 0) & (new_col < row_width)
    other_cell = new_row * row_width + jnp.clip(new_col, 0, row_width - 1)
    other_elem = elem_of_cell[other_cell]
    other_edge = (direction + 2 - turns[other_elem]) % 4
    same_half = (edge_ids < 2) == (other_edge < 2)
    linked = jnp.where(inside, other_elem, -1).astype(jnp.int32)
    linked_edge = jnp.where(inside, other_edge, 0).astype(jnp.int32)
    reversed_flag = jnp.where(inside & same_half, 1, 0).astype(jnp.int32)
    return (linked, linked_edge, reversed_flag)


def draw_neighbour(key, part):
    mesh_lists = build_mesh(key)
    return mesh_lists[0]


def draw_neighbour_edge(key, part):
    mesh_lists = build_mesh(key)
    return mesh_lists[1]


def draw_flipped(key, part):
    mesh_lists = build_mesh(key)
    return mesh_lists[2]


def draw_velocity_modes(key, part):
    key = jax.random.fold_in(key, 5)
    plane_ids = jnp.arange(PLANES)
    signed = jnp.abs(jnp.where(plane_ids < PLANES // 2, plane_ids, plane_ids - PLANES)).astype(jnp.float32)
    envelope = 0.35 / (1.0 + signed / 16.0) ** 2
    array_shape = (2, 3, PLANES, GRID_POINTS)
    raw_values = jnp.clip(jax.random.normal(key, array_shape, jnp.float32), -4.0, 4.0)
    return raw_values * envelope[None, None, :, None]


def levels(key, dims, cuts, smallest, top_value):
    loudness, own = 1.0, jax.random.fold_in(key, 6)
    for dim, blocks in cuts:
        draws = jnp.exp(jax.random.uniform(jax.random.fold_in(own, dim), (blocks,), jnp.float32, smallest / len(cuts), top_value / len(cuts)))
        loudness = loudness * jnp.repeat(draws, dims[dim] // blocks).reshape([-1 if axis == dim else 1 for axis in range(len(dims))])
    return loudness


def normal_values(stream_key, shape, width, reach, pieces=(), kind=jnp.bfloat16):
    gain = levels(stream_key, shape, pieces, -0.22, 0.18) if pieces else 1.0
    array = jax.random.normal(stream_key, shape, jnp.float32) * width * gain
    return jnp.minimum(jnp.maximum(array, -reach), reach).astype(kind)


def setup_inputs(seed: int = 0) -> dict:
    key_of = jax.random.split(jax.random.key(seed), 6)
    return {
        "velocity_modes": draw_velocity_modes(jax.random.fold_in(key_of[5], 71), 0),
        "geometry": normal_values(key_of[1], (4, GRID_POINTS), 1.0, 4.0, ((1, 16),), jnp.float32),
        "neighbour": draw_neighbour(jax.random.fold_in(key_of[5], 71), 0),
        "neighbour_edge": draw_neighbour_edge(jax.random.fold_in(key_of[5], 71), 0),
        "flipped": draw_flipped(jax.random.fold_in(key_of[5], 71), 0),
    }


span_wave = 2.0
highest = lax.Precision.HIGHEST
gll_nodes = [-1.0, -0.8717401485096066, -0.5917001814331423, -0.2092992179024789, 0.2092992179024789, 0.5917001814331423, 0.8717401485096066, 1.0]


def legendre_seven(point_value):
    earlier_value = 1.0
    current_value = point_value
    for degree_index in range(1, 7):
        next_value = ((2 * degree_index + 1) * point_value * current_value - degree_index * earlier_value) / (degree_index + 1)
        earlier_value = current_value
        current_value = next_value
    return current_value


def gll_matrices():
    legendre_vals = [legendre_seven(node_value) for node_value in gll_nodes]
    deriv_matrix = np.zeros((8, 8))
    for row_index in range(8):
        for col_index in range(8):
            if row_index != col_index:
                deriv_matrix[row_index, col_index] = legendre_vals[row_index] / legendre_vals[col_index] / (gll_nodes[row_index] - gll_nodes[col_index])
    deriv_matrix[0, 0] = -14.0
    deriv_matrix[7, 7] = 14.0
    identity = np.eye(8)
    return np.kron(identity, deriv_matrix), np.kron(deriv_matrix, identity)


def edge_interior(field):
    return jnp.stack([field[..., 0, 1:7], field[..., 1:7, 7], field[..., 7, 1:7], field[..., 1:7, 0]], axis=-2)


def put_edges(field, edges):
    field = field.at[..., 0, 1:7].set(edges[..., 0, :])
    field = field.at[..., 1:7, 7].set(edges[..., 1, :])
    field = field.at[..., 7, 1:7].set(edges[..., 2, :])
    return field.at[..., 1:7, 0].set(edges[..., 3, :])


def reference(velocity_modes, geometry, neighbour, neighbour_edge, flipped):
    xi_table, eta_table = gll_matrices()
    xi_matrix = jnp.asarray(xi_table, jnp.float32)
    eta_matrix = jnp.asarray(eta_table, jnp.float32)
    plane_ids = jnp.arange(PLANES, dtype=jnp.int32)
    signed = jnp.where(plane_ids < PLANES // 2, plane_ids, plane_ids - PLANES)
    wave_factor = (span_wave * signed.astype(jnp.float32))[None, :, None]
    span_modes = jnp.stack([-wave_factor * velocity_modes[1], wave_factor * velocity_modes[0]])
    spectral = jnp.concatenate([velocity_modes, span_modes], axis=1)
    physical = (PLANES * jnp.real(jnp.fft.ifft(spectral[0] + 1j * spectral[1], axis=1))).astype(jnp.float32)
    velocity = physical[:3].reshape(3, PLANES, ELEMENTS, POINTS)
    along_xi = jnp.einsum("fpeq,rq->fper", velocity, xi_matrix, precision=highest)
    along_eta = jnp.einsum("fpeq,rq->fper", velocity, eta_matrix, precision=highest)
    metric = geometry.reshape(4, ELEMENTS, POINTS)
    grad_x = metric[0] * along_xi + metric[1] * along_eta
    grad_y = metric[2] * along_xi + metric[3] * along_eta
    cells = jnp.stack([grad_x, grad_y], axis=1).reshape(6, PLANES, ELEMENTS, 8, 8)
    own_edges = edge_interior(cells)
    flat_edges = own_edges.reshape(6, PLANES, ELEMENTS * 4, 6)
    row_ids = (jnp.maximum(neighbour, 0) * 4 + neighbour_edge).reshape(-1)
    far_edges = jnp.take(flat_edges, row_ids, axis=2).reshape(6, PLANES, ELEMENTS, 4, 6)
    far_edges = jnp.where(flipped[:, :, None] == 1, far_edges[..., ::-1], far_edges)
    averaged = jnp.where(neighbour[:, :, None] >= 0, 0.5 * (own_edges + far_edges), own_edges)
    gradients = put_edges(cells, averaged).reshape(6, PLANES, GRID_POINTS)
    nonlinear = physical[0] * gradients[0::2] + physical[1] * gradients[1::2] + physical[2] * physical[3:]
    spectrum = jnp.fft.fft(nonlinear, axis=1) / PLANES
    return jnp.stack([jnp.real(spectrum), jnp.imag(spectrum)]).astype(jnp.float32)
```

```python
import jax
import jax.numpy as jnp
import ml_dtypes
import numpy as np
from jax import lax
from jax.experimental import pallas as pl
from jax.experimental.pallas import tpu as pltpu
from jax.sharding import PartitionSpec as P

PLANES = 1024
POINTS = 64
MESH = pl.DeviceIdType.MESH
highest = lax.Precision.HIGHEST
gll_nodes = [
    -1.0,
    -0.8717401485096066,
    -0.5917001814331423,
    -0.2092992179024789,
    0.2092992179024789,
    0.5917001814331423,
    0.8717401485096066,
    1.0,
]


def legendre_seven(point_value):
    earlier_value = 1.0
    current_value = point_value
    for degree_index in range(1, 7):
        next_value = (
            (2 * degree_index + 1) * point_value * current_value - degree_index * earlier_value
        ) / (degree_index + 1)
        earlier_value = current_value
        current_value = next_value
    return current_value


def gll_matrices():
    legendre_vals = [legendre_seven(node_value) for node_value in gll_nodes]
    deriv_matrix = np.zeros((8, 8))
    for row_index in range(8):
        for col_index in range(8):
            if row_index != col_index:
                deriv_matrix[row_index, col_index] = (
                    legendre_vals[row_index]
                    / legendre_vals[col_index]
                    / (gll_nodes[row_index] - gll_nodes[col_index])
                )
    deriv_matrix[0, 0] = -14.0
    deriv_matrix[7, 7] = 14.0
    identity = np.eye(8)
    return (np.kron(identity, deriv_matrix), np.kron(deriv_matrix, identity))


def halves(matrix):
    high = matrix.astype(ml_dtypes.bfloat16)
    low = (matrix - high.astype(np.float64)).astype(ml_dtypes.bfloat16)
    return high, low


def point_order():
    steps = range(1, 7)
    order = [p for p in steps] + [8 * p + 7 for p in steps]
    order += [56 + p for p in steps] + [8 * p for p in steps]
    return order + [r for r in range(POINTS) if r not in order]


def tables():
    order = point_order()
    xi, eta = gll_matrices()
    eye = np.eye(POINTS)[order]
    pair = np.kron(np.eye(2), eye)
    edge_xi = np.kron(np.eye(2), xi[order[:24]])
    edge_eta = np.kron(np.eye(2), eta[order[:24]])
    pack_high, pack_low = halves(np.concatenate([pair, edge_xi, edge_eta]))
    pack_low = pack_low[128:]
    edge_pick = np.kron(np.eye(2), eye[:24]).astype(np.float32)

    k = (64 * np.arange(8)[:, None] + np.arange(64)[None, :])[:, None, :]
    waves = []
    for block in range(4):
        plane = 2 * (256 * (block % 2) + np.arange(256)) + block // 2
        angle = (k[..., None] * plane) % PLANES * (2.0 * np.pi / PLANES)
        waves.append(np.concatenate([np.cos(angle), -np.sin(angle)], axis=1).reshape(1024, 256))
    wave_high, wave_low = halves(np.stack(waves))

    mode = 64 * np.arange(16)[:, None] + np.arange(64)[None, :]
    factor = 2.0 * np.where(mode < 512, mode, mode - 1024)
    factor = np.concatenate([-factor, factor], axis=1).astype(np.float32)[:, None, :]

    own_xi = xi[order][:, order].astype(np.float32)
    own_eta = eta[order][:, order].astype(np.float32)

    row = np.arange(384)
    owner = (row[:, None] // 24 == np.arange(16)).astype(np.float32)
    edge = (row[:, None] % 24 // 6 == np.arange(4)).astype(np.float32)
    place = (row % 6).astype(np.float32)[:, None]
    edge_own = np.concatenate([edge[:24], np.zeros((40, 4), np.float32)])

    def unpack(points):
        out = np.zeros((2, 3, len(points), 3, 128))
        for side in range(2):
            for field in range(3):
                for r, point in enumerate(points):
                    out[side, field, r, field, 64 * side + point] = 1.0
        return out.reshape(6 * len(points), 384).astype(ml_dtypes.bfloat16)

    return dict(
        pack_high=pack_high,
        pack_low=pack_low,
        edge_pick=edge_pick,
        pair=pair.astype(np.float32),
        factor=factor,
        own_xi=own_xi,
        own_eta=own_eta,
        owner=owner,
        edge=edge,
        place=place,
        edge_own=edge_own,
        unpack_edge=unpack(order[:24]),
        unpack_rest=unpack(order[24:]),
        wave_high=wave_high,
        wave_low=wave_low,
    )


def split(x):
    high = x.astype(jnp.bfloat16)
    return high, (x - high.astype(jnp.float32)).astype(jnp.bfloat16)


def mm(a, b, dims=((1,), (0,))):
    return lax.dot_general(a, b, (dims, ((), ())), preferred_element_type=jnp.float32)


NT = ((1,), (1,))
TN = ((0,), (0,))


def mm3(a, b, dims=((1,), (0,))):
    return mm(a[0], b[0], dims) + (mm(a[0], b[1], dims) + mm(a[1], b[0], dims))


def exact(a, b, dims=((1,), (0,))):
    return lax.dot_general(
        a, b, (dims, ((), ())), precision=highest, preferred_element_type=jnp.float32
    )


def kernel(
    modes, geometry, neighbour, neighbour_edge, flipped,
    pack_high, pack_low, edge_pick, pair, factor, own_xi, own_eta, owner, edge, place, edge_own,
    unpack_edge, unpack_rest, wave_high_hbm, wave_low_hbm,
    out,
    wave_high, wave_low, geo_column, send_vel, recv_vel, traces, far, recv_far, left_high, left_low,
    left_edge, rest, own_edge, uv_edge, total_rest, total_edge, send_rest, recv_rest, send_edge, recv_edge,
    wave_sem, trace_send, trace_recv, vel_s, vel_r, far_s, far_r, rest_s, rest_r, edge_s, edge_r,
):
    me = lax.axis_index("plane")
    group = lax.axis_index("elem")
    z = me // 2
    x = me % 2

    def peer(i):
        h = i // 2
        dz = (h + 1) // 2 * (2 * (h % 2) - 1)
        return (z + dz + 8) % 8 * 2 + (x + i) % 2

    loads = [
        pltpu.make_async_copy(wave_high_hbm, wave_high, wave_sem.at[0]),
        pltpu.make_async_copy(wave_low_hbm, wave_low, wave_sem.at[1]),
    ]
    for load in loads:
        load.start()

    barrier = pltpu.get_barrier_semaphore()

    def greet(i, carry):
        pl.semaphore_signal(barrier, inc=1, device_id={"plane": peer(i)}, device_id_type=MESH)
        return carry

    lax.fori_loop(1, 16, greet, 0)
    before = (group + 15) % 16
    after = (group + 1) % 16
    for other in (before, after):
        pl.semaphore_signal(barrier, inc=1, device_id={"elem": other}, device_id_type=MESH)
    pl.semaphore_wait(barrier, 17)

    def pack(q):
        cols = pl.ds(pl.multiple_of(128 * q, 128), 128)
        block = jnp.concatenate(
            [modes[c, f, :, cols] for f in range(3) for c in range(2)], axis=0
        )
        high, low = split(block)
        both = mm(pack_high[...], high, NT) + mm(pack_high[...], low, NT)
        send_vel[q] = both[:128]
        along = both[128:] + mm(pack_low[...], high, NT)
        geo = exact(edge_pick[...], geometry[:, cols], NT)
        rows = pl.ds(pl.multiple_of(48 * q, 16), 48)
        traces[rows, :384] = geo[:, 0:1] * along[:48] + geo[:, 1:2] * along[48:]
        traces[rows, 384:] = geo[:, 2:3] * along[:48] + geo[:, 3:4] * along[48:]

    def vel_part(p):
        return send_vel.at[p // 2, pl.ds(pl.multiple_of(p % 2 * 64, 64), 64)]

    def vel_copy(p, slot):
        return pltpu.make_async_remote_copy(
            vel_part(p), recv_vel.at[slot], vel_s.at[p], vel_r.at[slot],
            device_id={"plane": p}, device_id_type=MESH,
        )

    pack(z)
    vel_copy(peer(1), me).start()
    recv_vel[me] = send_vel[z, pl.ds(pl.multiple_of(x * 64, 64), 64), :]

    def pack_step(h, carry):
        pack(peer(2 * h) // 2)
        vel_copy(peer(2 * h), me).start()
        vel_copy(peer(2 * h + 1), me).start()
        return carry

    lax.fori_loop(1, 8, pack_step, 0)

    def trace_copy(slot, other):
        return pltpu.make_async_remote_copy(
            traces.at[pl.ds(0, 384)], traces.at[pl.ds(384 * (slot + 1), 384)],
            trace_send.at[slot], trace_recv.at[slot],
            device_id={"elem": other}, device_id_type=MESH,
        )

    trace_copies = [trace_copy(0, after), trace_copy(1, before)]
    for copy in trace_copies:
        copy.start()

    near = jnp.maximum(neighbour[...], 0)
    offset = lax.rem(lax.shift_right_logical(near, 4) - group + 16, 16)
    where = jnp.where(offset == 0, 0, jnp.where(offset == 1, 2, 1))
    start = where * 384 + (near & 15) * 24 + neighbour_edge[...] * 6 + flipped[...] * 5
    start = jnp.where(neighbour[...] >= 0, start, -5000).astype(jnp.float32)
    turn = (1 - 2 * flipped[...]).astype(jnp.float32)
    start = jnp.sum(exact(owner[...], start) * edge[...], axis=1, keepdims=True)
    turn = jnp.sum(exact(owner[...], turn) * edge[...], axis=1, keepdims=True)
    target = start + turn * place[...]
    source = lax.broadcasted_iota(jnp.int32, (384, 1152), 1).astype(jnp.float32)
    pick = jnp.where(source == target, 0.5, 0.0).astype(jnp.bfloat16)

    geo_column[...] = exact(pair[...], geometry[:, pl.ds(pl.multiple_of(128 * z, 128), 128)], NT)
    geo = geo_column[pl.ds(pl.multiple_of(64 * x, 64), 64), :]
    joined = jnp.where(neighbour[pl.ds(me, 1), :] >= 0, 0.5, 0.0)
    keep = 1.0 - jnp.sum(edge_own[...] * joined, axis=1, keepdims=True)
    to_x = keep * (geo[:, 0:1] * own_xi[...] + geo[:, 1:2] * own_eta[...])
    to_y = keep * (geo[:, 2:3] * own_xi[...] + geo[:, 3:4] * own_eta[...])
    gradient = split(jnp.concatenate([to_x, to_y], axis=0))

    for copy in trace_copies:
        copy.wait_recv()

    for j in range(3):
        high, low = split(traces[:, 256 * j : 256 * j + 256])
        far[:, 256 * j : 256 * j + 256] = mm(pick, high) + mm(pick, low)

    def far_part(p):
        return far.at[pl.ds(pl.multiple_of(24 * p, 8), 24)]

    def far_copy(p, slot):
        return pltpu.make_async_remote_copy(
            far_part(p), recv_far.at[slot], far_s.at[p], far_r.at[slot],
            device_id={"plane": p}, device_id_type=MESH,
        )

    def far_step(i, carry):
        far_copy(peer(i), me).start()
        return carry

    lax.fori_loop(1, 16, far_step, 0)
    recv_far[me] = far[pl.ds(pl.multiple_of(24 * me, 8), 24), :]

    def vel_wait(i, carry):
        vel_copy(peer(i), peer(i)).wait_recv()
        return carry

    lax.fori_loop(1, 16, vel_wait, 0)

    def gather(a, carry):
        lanes = pl.ds(pl.multiple_of(128 * a, 128), 128)
        for f in range(3):
            one = recv_vel[a, :, 128 * f : 128 * f + 128]
            two = recv_vel[a + 8, :, 128 * f : 128 * f + 128]
            one_z = pltpu.roll(one, 64, 1) * factor[a]
            two_z = pltpu.roll(two, 64, 1) * factor[a + 8]
            for r, (p, q) in enumerate(((one, two), (one_z, two_z))):
                rows = slice(192 * r + 64 * f, 192 * r + 64 * f + 64)
                high, low = split(p + q)
                left_high[0, rows, lanes] = high
                left_low[0, rows, lanes] = low
                high, low = split(p - q)
                left_high[1, rows, lanes] = high
                left_low[1, rows, lanes] = low
        return carry

    lax.fori_loop(0, 8, gather, 0)
    for load in loads:
        load.wait()

    total_rest[...] = jnp.zeros_like(total_rest)
    total_edge[...] = jnp.zeros_like(total_edge)

    def planes(n, carry):
        parity = n // 2
        waves = (wave_high[n], wave_low[n])
        physical = mm3((left_high[parity], left_low[parity]), waves)
        u, v, w = physical[:64], physical[64:128], physical[128:192]
        uv_edge[n, :24] = u[:24]
        uv_edge[n, 24:] = v[:24]
        for f, field in enumerate((u, v, w)):
            slopes = mm3(gradient, split(field))
            spanwise = physical[192 + 64 * f : 256 + 64 * f]
            product = u * slopes[:64] + v * slopes[64:] + w * spanwise
            own_edge[n, 24 * f : 24 * f + 24] = product[:24]
            rest[40 * f : 40 * f + 40] = product[24:]
        total_rest[parity] += mm3(split(rest[...]), waves, NT)
        return carry

    lax.fori_loop(0, 4, planes, 0)

    def combine(total, send):
        for a in range(8):
            even = total[0, :, 128 * a : 128 * a + 128]
            odd = total[1, :, 128 * a : 128 * a + 128]
            send[a] = (even + odd) * (1.0 / PLANES)
            send[a + 8] = (even - odd) * (1.0 / PLANES)

    def back_copy(send, recv, send_sem, recv_sem, p, slot):
        return pltpu.make_async_remote_copy(
            send.at[p], recv.at[slot], send_sem.at[p], recv_sem.at[slot],
            device_id={"plane": p}, device_id_type=MESH,
        )

    def back(total, send, recv, send_sem, recv_sem):
        combine(total, send)

        def step(i, carry):
            back_copy(send, recv, send_sem, recv_sem, peer(i), me).start()
            return carry

        lax.fori_loop(1, 16, step, 0)
        recv[me] = send[me]

    back(total_rest, send_rest, recv_rest, rest_s, rest_r)

    def far_wait(i, carry):
        far_copy(peer(i), peer(i)).wait_recv()
        return carry

    lax.fori_loop(1, 16, far_wait, 0)

    def gather_far(a, carry):
        lanes = pl.ds(pl.multiple_of(128 * a, 128), 128)
        for g in range(6):
            one = recv_far[a, :, 128 * g : 128 * g + 128]
            two = recv_far[a + 8, :, 128 * g : 128 * g + 128]
            left_edge[0, 24 * g : 24 * g + 24, lanes] = one + two
            left_edge[1, 24 * g : 24 * g + 24, lanes] = one - two
        return carry

    lax.fori_loop(0, 8, gather_far, 0)

    def edges(n, carry):
        parity = n // 2
        waves = (wave_high[n], wave_low[n])
        slopes = mm3(split(left_edge[parity]), waves)
        u, v = uv_edge[n, :24], uv_edge[n, 24:]
        product = jnp.concatenate(
            [
                own_edge[n, 24 * f : 24 * f + 24]
                + u * slopes[24 * f : 24 * f + 24]
                + v * slopes[72 + 24 * f : 96 + 24 * f]
                for f in range(3)
            ],
            axis=0,
        )
        total_edge[parity] += mm3(split(product), waves, NT)
        return carry

    lax.fori_loop(0, 4, edges, 0)
    back(total_edge, send_edge, recv_edge, edge_s, edge_r)

    def back_wait(recv, send, send_sem, recv_sem):
        def step(i, carry):
            back_copy(send, recv, send_sem, recv_sem, peer(i), peer(i)).wait_recv()
            return carry

        lax.fori_loop(1, 16, step, 0)

    def unpack(recv, table, add):
        def step(q, carry):
            cols = pl.ds(pl.multiple_of(128 * q, 128), 128)
            high, low = split(jnp.concatenate([recv[2 * q], recv[2 * q + 1]], axis=0))
            turned = mm(high, table[...], TN) + mm(low, table[...], TN)
            for c in range(2):
                for f in range(3):
                    part = turned[64 * c : 64 * c + 64, 128 * f : 128 * f + 128]
                    if add:
                        part = part + out[c, f, :, cols]
                    out[c, f, :, cols] = part
            return carry

        lax.fori_loop(0, 8, step, 0)

    back_wait(recv_rest, send_rest, rest_s, rest_r)
    unpack(recv_rest, unpack_rest, False)
    back_wait(recv_edge, send_edge, edge_s, edge_r)
    unpack(recv_edge, unpack_edge, True)

    def drain(i, carry):
        p = peer(i)
        vel_copy(p, me).wait_send()
        far_copy(p, me).wait_send()
        back_copy(send_rest, recv_rest, rest_s, rest_r, p, me).wait_send()
        back_copy(send_edge, recv_edge, edge_s, edge_r, p, me).wait_send()
        return carry

    lax.fori_loop(1, 16, drain, 0)
    for copy in trace_copies:
        copy.wait_send()


def shards(velocity_modes, geometry, neighbour, neighbour_edge, flipped):
    names = tables()
    constants = [jnp.asarray(value) for value in names.values()]
    vmem = pl.BlockSpec(memory_space=pltpu.VMEM)
    anywhere = pl.BlockSpec(memory_space=pl.ANY)
    f32 = jnp.float32
    return pl.pallas_call(
        kernel,
        out_shape=jax.ShapeDtypeStruct(velocity_modes.shape, f32),
        in_specs=[vmem] * (5 + len(constants) - 2) + [anywhere] * 2,
        out_specs=vmem,
        scratch_shapes=[
            pltpu.VMEM((4, 1024, 256), jnp.bfloat16),
            pltpu.VMEM((4, 1024, 256), jnp.bfloat16),
            pltpu.VMEM((128, 4), f32),
            pltpu.VMEM((8, 128, 384), f32),
            pltpu.VMEM((16, 64, 384), f32),
            pltpu.VMEM((1152, 768), f32),
            pltpu.VMEM((384, 768), f32),
            pltpu.VMEM((16, 24, 768), f32),
            pltpu.VMEM((2, 384, 1024), jnp.bfloat16),
            pltpu.VMEM((2, 384, 1024), jnp.bfloat16),
            pltpu.VMEM((2, 144, 1024), f32),
            pltpu.VMEM((120, 256), f32),
            pltpu.VMEM((4, 72, 256), f32),
            pltpu.VMEM((4, 48, 256), f32),
            pltpu.VMEM((2, 120, 1024), f32),
            pltpu.VMEM((2, 72, 1024), f32),
            pltpu.VMEM((16, 120, 128), f32),
            pltpu.VMEM((16, 120, 128), f32),
            pltpu.VMEM((16, 72, 128), f32),
            pltpu.VMEM((16, 72, 128), f32),
            pltpu.SemaphoreType.DMA((2,)),
            pltpu.SemaphoreType.DMA((2,)),
            pltpu.SemaphoreType.DMA((2,)),
        ]
        + [pltpu.SemaphoreType.DMA((16,))] * 8,
        compiler_params=pltpu.CompilerParams(
            collective_id=0, has_side_effects=True, vmem_limit_bytes=56 * 2**20
        ),
    )(velocity_modes, geometry, neighbour, neighbour_edge, flipped, *constants)


def solution(mesh):
    placed = (
        P(None, None, "plane", "elem"),
        P(None, "elem"),
        P("elem", None),
        P("elem", None),
        P("elem", None),
    )
    return jax.shard_map(
        shards,
        mesh=mesh,
        in_specs=placed,
        out_specs=P(None, None, "plane", "elem"),
        check_vma=False,
    )
```

```python
import jax
import jax.numpy as jnp
import ml_dtypes
import numpy as np
from jax import lax
from jax.experimental import pallas as pl
from jax.experimental.pallas import tpu as pltpu
from jax.sharding import PartitionSpec as P

PLANES = 1024
POINTS = 64
MESH = pl.DeviceIdType.MESH
highest = lax.Precision.HIGHEST
gll_nodes = [
    -1.0,
    -0.8717401485096066,
    -0.5917001814331423,
    -0.2092992179024789,
    0.2092992179024789,
    0.5917001814331423,
    0.8717401485096066,
    1.0,
]


def legendre_seven(point_value):
    earlier_value = 1.0
    current_value = point_value
    for degree_index in range(1, 7):
        next_value = (
            (2 * degree_index + 1) * point_value * current_value - degree_index * earlier_value
        ) / (degree_index + 1)
        earlier_value = current_value
        current_value = next_value
    return current_value


def gll_matrices():
    legendre_vals = [legendre_seven(node_value) for node_value in gll_nodes]
    deriv_matrix = np.zeros((8, 8))
    for row_index in range(8):
        for col_index in range(8):
            if row_index != col_index:
                deriv_matrix[row_index, col_index] = (
                    legendre_vals[row_index]
                    / legendre_vals[col_index]
                    / (gll_nodes[row_index] - gll_nodes[col_index])
                )
    deriv_matrix[0, 0] = -14.0
    deriv_matrix[7, 7] = 14.0
    identity = np.eye(8)
    return (np.kron(identity, deriv_matrix), np.kron(deriv_matrix, identity))


def halves(matrix):
    high = matrix.astype(ml_dtypes.bfloat16)
    low = (matrix - high.astype(np.float64)).astype(ml_dtypes.bfloat16)
    return high, low


def point_order():
    steps = range(1, 7)
    order = [p for p in steps] + [8 * p + 7 for p in steps]
    order += [56 + p for p in steps] + [8 * p for p in steps]
    return order + [r for r in range(POINTS) if r not in order]


def tables():
    order = point_order()
    xi, eta = gll_matrices()
    eye = np.eye(POINTS)[order]
    pair = np.kron(np.eye(2), eye)
    edge_xi = np.kron(np.eye(2), xi[order[:24]])
    edge_eta = np.kron(np.eye(2), eta[order[:24]])
    pack_high, pack_low = halves(np.concatenate([pair, edge_xi, edge_eta]))
    pack = np.concatenate([pack_high, pack_low[128:]])

    k = (64 * np.arange(8)[:, None] + np.arange(64)[None, :])[:, None, :]
    waves = []
    for block in range(4):
        plane = 2 * (256 * (block % 2) + np.arange(256)) + block // 2
        angle = (k[..., None] * plane) % PLANES * (2.0 * np.pi / PLANES)
        waves.append(np.concatenate([np.cos(angle), -np.sin(angle)], axis=1).reshape(1024, 256))
    wave = np.stack(halves(np.stack(waves)))

    mode = 64 * np.arange(16)[:, None] + np.arange(64)[None, :]
    factor = 2.0 * np.where(mode < 512, mode, mode - 1024)
    dense = np.zeros((144, 128), np.float32)
    dense[:64, :64] = xi[order][:, order]
    dense[64:128, :64] = eta[order][:, order]
    dense[128:] = np.concatenate([-factor, factor], axis=1)

    def unpack(points):
        out = np.zeros((2, 3, len(points), 3, 128))
        for side in range(2):
            for field in range(3):
                for r, point in enumerate(points):
                    out[side, field, r, field, 64 * side + point] = 1.0
        return out.reshape(6 * len(points), 384).astype(ml_dtypes.bfloat16)

    turn = np.concatenate([unpack(order[:24]), unpack(order[24:])])
    return pack, dense, turn, wave


def split(x):
    high = x.astype(jnp.bfloat16)
    return high, (x - high.astype(jnp.float32)).astype(jnp.bfloat16)


def mm(a, b, dims=((1,), (0,))):
    return lax.dot_general(a, b, (dims, ((), ())), preferred_element_type=jnp.float32)


NT = ((1,), (1,))
TN = ((0,), (0,))


def mm3(a, b, dims=((1,), (0,))):
    return mm(a[0], b[0], dims) + (mm(a[0], b[1], dims) + mm(a[1], b[0], dims))


def exact(a, b, dims=((1,), (0,))):
    return lax.dot_general(
        a, b, (dims, ((), ())), precision=highest, preferred_element_type=jnp.float32
    )


def kernel(
    modes_hbm, geometry_hbm, neighbour_hbm, neighbour_edge_hbm, flipped_hbm,
    pack_hbm, dense_hbm, turn_hbm, wave_hbm,
    out_hbm,
    modes, geometry, neighbour, neighbour_edge, flipped, pack_table, dense, turn_table, wave, out,
    geo_column, send_vel, recv_vel, traces, far, recv_far, left_high, left_low,
    left_edge, rest, own_edge, uv_edge, total_rest, total_edge, send_rest, recv_rest, send_edge, recv_edge,
    load_sem, mode_sem, out_sem,
    trace_send, trace_recv, vel_s, vel_r, far_s, far_r, rest_s, rest_r, edge_s, edge_r,
):
    me = lax.axis_index("plane")
    group = lax.axis_index("elem")
    z = me // 2
    x = me % 2

    def peer(i):
        h = i // 2
        dz = (h + 1) // 2 * (2 * (h % 2) - 1)
        return (z + dz + 8) % 8 * 2 + (x + i) % 2

    barrier = pltpu.get_barrier_semaphore()

    def greet(i, carry):
        pl.semaphore_signal(barrier, inc=1, device_id={"plane": peer(i)}, device_id_type=MESH)
        return carry

    lax.fori_loop(1, 16, greet, 0)
    before = (group + 15) % 16
    after = (group + 1) % 16
    for other in (before, after):
        pl.semaphore_signal(barrier, inc=1, device_id={"elem": other}, device_id_type=MESH)

    def pair_cols(q):
        return pl.ds(pl.multiple_of(128 * q, 128), 128)

    def mode_load(q):
        return pltpu.make_async_copy(modes_hbm.at[:, :, :, pair_cols(q)], modes.at[q], mode_sem.at[q])

    loads = [
        pltpu.make_async_copy(source, target, load_sem.at[i])
        for i, (source, target) in enumerate((
            (pack_hbm, pack_table),
            (geometry_hbm, geometry),
            (neighbour_hbm, neighbour),
            (neighbour_edge_hbm, neighbour_edge),
            (flipped_hbm, flipped),
            (dense_hbm, dense),
            (wave_hbm, wave),
            (turn_hbm, turn_table),
        ))
    ]
    loads[0].start()
    mode_load(peer(2) // 2).start()
    loads[1].start()

    def mode_start(h, carry):
        mode_load(peer(2 * h) // 2).start()
        return carry

    lax.fori_loop(2, 8, mode_start, 0)
    mode_load(z).start()
    for load in loads[2:]:
        load.start()

    def pack(q):
        mode_load(q).wait()
        block = jnp.concatenate([modes[q, c, f] for f in range(3) for c in range(2)], axis=0)
        high, low = split(block)
        both = mm(pack_table[:224], high, NT) + mm(pack_table[:224], low, NT)
        send_vel[q] = both[:128]
        along = both[128:] + mm(pack_table[224:], high, NT)
        pick = jnp.concatenate([pack_table[:24], pack_table[64:88]], axis=0).astype(jnp.float32)
        geo = exact(pick, geometry[:, pair_cols(q)], NT)
        rows = pl.ds(pl.multiple_of(48 * q, 16), 48)
        traces[rows, :384] = geo[:, 0:1] * along[:48] + geo[:, 1:2] * along[48:]
        traces[rows, 384:] = geo[:, 2:3] * along[:48] + geo[:, 3:4] * along[48:]

    def vel_part(p):
        return send_vel.at[p // 2, pl.ds(pl.multiple_of(p % 2 * 64, 64), 64)]

    def vel_copy(p, slot):
        return pltpu.make_async_remote_copy(
            vel_part(p), recv_vel.at[slot], vel_s.at[p], vel_r.at[slot],
            device_id={"plane": p}, device_id_type=MESH,
        )

    loads[0].wait()
    loads[1].wait()
    pack(peer(2) // 2)
    pl.semaphore_wait(barrier, 17)
    vel_copy(peer(2), me).start()
    vel_copy(peer(3), me).start()

    def pack_step(h, carry):
        pack(peer(2 * h) // 2)
        vel_copy(peer(2 * h), me).start()
        vel_copy(peer(2 * h + 1), me).start()
        return carry

    lax.fori_loop(2, 8, pack_step, 0)
    pack(z)
    vel_copy(peer(1), me).start()
    recv_vel[me] = send_vel[z, pl.ds(pl.multiple_of(x * 64, 64), 64), :]

    def trace_copy(slot, other):
        return pltpu.make_async_remote_copy(
            traces.at[pl.ds(0, 384)], traces.at[pl.ds(384 * (slot + 1), 384)],
            trace_send.at[slot], trace_recv.at[slot],
            device_id={"elem": other}, device_id_type=MESH,
        )

    trace_copies = [trace_copy(0, after), trace_copy(1, before)]
    for copy in trace_copies:
        copy.start()

    for load in loads[2:6]:
        load.wait()

    def iota(shape, axis):
        return lax.broadcasted_iota(jnp.int32, shape, axis)

    def rows_of(shape):
        row = iota(shape, 0)
        element = (row * 2731) >> 16
        edge = ((row - element * 24) * 10923) >> 16
        return element, edge, row - element * 24 - edge * 6

    near = jnp.maximum(neighbour[...], 0)
    offset = ((near >> 4) - group + 16) & 15
    where = jnp.where(offset == 0, 0, jnp.where(offset == 1, 2, 1))
    start = where * 384 + (near & 15) * 24 + neighbour_edge[...] * 6 + flipped[...] * 5
    start = jnp.where(neighbour[...] >= 0, start, -5000).astype(jnp.float32)
    turn = (1 - 2 * flipped[...]).astype(jnp.float32)
    owner = (rows_of((384, 16))[0] == iota((384, 16), 1)).astype(jnp.float32)
    edge = (rows_of((384, 4))[1] == iota((384, 4), 1)).astype(jnp.float32)
    place = rows_of((384, 1))[2].astype(jnp.float32)
    start = jnp.sum(exact(owner, start, NT) * edge, axis=1, keepdims=True)
    turn = jnp.sum(exact(owner, turn, NT) * edge, axis=1, keepdims=True)
    target = start + turn * place
    pick = jnp.where(iota((384, 1152), 1).astype(jnp.float32) == target, 0.5, 0.0)
    pick = pick.astype(jnp.bfloat16)

    geo_column[...] = exact(pack_table[:128].astype(jnp.float32), geometry[:, pair_cols(z)], NT)
    geo = geo_column[pl.ds(pl.multiple_of(64 * x, 64), 64), :]
    joined = jnp.where(neighbour[...] >= 0, 0.5, 0.0)
    edge_own = (rows_of((64, 4))[1] + 4 * rows_of((64, 4))[0] == iota((64, 4), 1))
    joined = exact(edge_own.astype(jnp.float32), joined)
    joined = jnp.where(iota((64, 16), 1) == me, joined, 0.0)
    keep = 1.0 - jnp.sum(joined, axis=1, keepdims=True)
    own_xi, own_eta = dense[:64, :64], dense[64:128, :64]
    to_x = keep * (geo[:, 0:1] * own_xi + geo[:, 1:2] * own_eta)
    to_y = keep * (geo[:, 2:3] * own_xi + geo[:, 3:4] * own_eta)
    gradient = split(jnp.concatenate([to_x, to_y], axis=0))

    for copy in trace_copies:
        copy.wait_recv()

    for j in range(3):
        high, low = split(traces[:, 256 * j : 256 * j + 256])
        far[:, 256 * j : 256 * j + 256] = mm(pick, high) + mm(pick, low)

    def far_part(p):
        return far.at[pl.ds(pl.multiple_of(24 * p, 8), 24)]

    def far_copy(p, slot):
        return pltpu.make_async_remote_copy(
            far_part(p), recv_far.at[slot], far_s.at[p], far_r.at[slot],
            device_id={"plane": p}, device_id_type=MESH,
        )

    def far_step(i, carry):
        far_copy(peer(i), me).start()
        return carry

    lax.fori_loop(1, 16, far_step, 0)
    recv_far[me] = far[pl.ds(pl.multiple_of(24 * me, 8), 24), :]

    def vel_wait(i, carry):
        vel_copy(peer(i), peer(i)).wait_recv()
        return carry

    lax.fori_loop(1, 16, vel_wait, 0)

    def gather(a, carry):
        lanes = pl.ds(pl.multiple_of(128 * a, 128), 128)
        for f in range(3):
            one = recv_vel[a, :, 128 * f : 128 * f + 128]
            two = recv_vel[a + 8, :, 128 * f : 128 * f + 128]
            one_z = pltpu.roll(one, 64, 1) * dense[pl.ds(128 + a, 1), :]
            two_z = pltpu.roll(two, 64, 1) * dense[pl.ds(136 + a, 1), :]
            for r, (p, q) in enumerate(((one, two), (one_z, two_z))):
                rows = slice(192 * r + 64 * f, 192 * r + 64 * f + 64)
                high, low = split(p + q)
                left_high[0, rows, lanes] = high
                left_low[0, rows, lanes] = low
                high, low = split(p - q)
                left_high[1, rows, lanes] = high
                left_low[1, rows, lanes] = low
        return carry

    lax.fori_loop(0, 8, gather, 0)
    for load in loads[6:]:
        load.wait()

    total_rest[...] = jnp.zeros_like(total_rest)
    total_edge[...] = jnp.zeros_like(total_edge)

    def planes(n, carry):
        parity = n // 2
        waves = (wave[0, n], wave[1, n])
        physical = mm3((left_high[parity], left_low[parity]), waves)
        u, v, w = physical[:64], physical[64:128], physical[128:192]
        uv_edge[n, :24] = u[:24]
        uv_edge[n, 24:] = v[:24]
        for f, field in enumerate((u, v, w)):
            slopes = mm3(gradient, split(field))
            spanwise = physical[192 + 64 * f : 256 + 64 * f]
            product = u * slopes[:64] + v * slopes[64:] + w * spanwise
            own_edge[n, 24 * f : 24 * f + 24] = product[:24]
            rest[40 * f : 40 * f + 40] = product[24:]
        total_rest[parity] += mm3(split(rest[...]), waves, NT)
        return carry

    lax.fori_loop(0, 4, planes, 0)

    def combine(total, send):
        for a in range(8):
            even = total[0, :, 128 * a : 128 * a + 128]
            odd = total[1, :, 128 * a : 128 * a + 128]
            send[a] = (even + odd) * (1.0 / PLANES)
            send[a + 8] = (even - odd) * (1.0 / PLANES)

    def back_copy(send, recv, send_sem, recv_sem, p, slot):
        return pltpu.make_async_remote_copy(
            send.at[p], recv.at[slot], send_sem.at[p], recv_sem.at[slot],
            device_id={"plane": p}, device_id_type=MESH,
        )

    def back(total, send, recv, send_sem, recv_sem):
        combine(total, send)

        def step(i, carry):
            back_copy(send, recv, send_sem, recv_sem, peer(i), me).start()
            return carry

        lax.fori_loop(1, 16, step, 0)
        recv[me] = send[me]

    back(total_rest, send_rest, recv_rest, rest_s, rest_r)

    def far_wait(i, carry):
        far_copy(peer(i), peer(i)).wait_recv()
        return carry

    lax.fori_loop(1, 16, far_wait, 0)

    def gather_far(a, carry):
        lanes = pl.ds(pl.multiple_of(128 * a, 128), 128)
        for g in range(6):
            one = recv_far[a, :, 128 * g : 128 * g + 128]
            two = recv_far[a + 8, :, 128 * g : 128 * g + 128]
            left_edge[0, 24 * g : 24 * g + 24, lanes] = one + two
            left_edge[1, 24 * g : 24 * g + 24, lanes] = one - two
        return carry

    lax.fori_loop(0, 8, gather_far, 0)

    def edges(n, carry):
        parity = n // 2
        waves = (wave[0, n], wave[1, n])
        slopes = mm3(split(left_edge[parity]), waves)
        u, v = uv_edge[n, :24], uv_edge[n, 24:]
        product = jnp.concatenate(
            [
                own_edge[n, 24 * f : 24 * f + 24]
                + u * slopes[24 * f : 24 * f + 24]
                + v * slopes[72 + 24 * f : 96 + 24 * f]
                for f in range(3)
            ],
            axis=0,
        )
        total_edge[parity] += mm3(split(product), waves, NT)
        return carry

    lax.fori_loop(0, 4, edges, 0)
    back(total_edge, send_edge, recv_edge, edge_s, edge_r)

    def out_copy(q):
        return pltpu.make_async_copy(out.at[q], out_hbm.at[:, :, :, pair_cols(q)], out_sem.at[q])

    def unpack(q, recv, rows, add):
        high, low = split(jnp.concatenate([recv[2 * q], recv[2 * q + 1]], axis=0))
        turned = mm(high, turn_table[rows], TN) + mm(low, turn_table[rows], TN)
        for c in range(2):
            for f in range(3):
                part = turned[64 * c : 64 * c + 64, 128 * f : 128 * f + 128]
                if add:
                    part = part + out[q, c, f]
                out[q, c, f] = part
        if add:
            out_copy(q).start()

    def unpack_all(send, recv, send_sem, recv_sem, rows, add):
        def arrive(i):
            back_copy(send, recv, send_sem, recv_sem, peer(i), peer(i)).wait_recv()

        def step(h, carry):
            arrive(2 * h)
            arrive(2 * h + 1)
            unpack(peer(2 * h) // 2, recv, rows, add)
            return carry

        arrive(1)
        unpack(z, recv, rows, add)
        lax.fori_loop(1, 8, step, 0)

    unpack_all(send_rest, recv_rest, rest_s, rest_r, slice(144, 384), False)
    unpack_all(send_edge, recv_edge, edge_s, edge_r, slice(0, 144), True)

    def drain(i, carry):
        p = peer(i)
        vel_copy(p, me).wait_send()
        far_copy(p, me).wait_send()
        back_copy(send_rest, recv_rest, rest_s, rest_r, p, me).wait_send()
        back_copy(send_edge, recv_edge, edge_s, edge_r, p, me).wait_send()
        return carry

    lax.fori_loop(1, 16, drain, 0)
    for copy in trace_copies:
        copy.wait_send()
    for q in range(8):
        out_copy(q).wait()


def shards(velocity_modes, geometry, neighbour, neighbour_edge, flipped):
    constants = [jnp.asarray(value) for value in tables()]
    anywhere = pl.BlockSpec(memory_space=pl.ANY)
    f32 = jnp.float32
    operands = (velocity_modes, geometry, neighbour.T, neighbour_edge.T, flipped.T, *constants)
    return pl.pallas_call(
        kernel,
        out_shape=jax.ShapeDtypeStruct(velocity_modes.shape, f32),
        in_specs=[anywhere] * len(operands),
        out_specs=anywhere,
        scratch_shapes=[
            pltpu.VMEM((8, 2, 3, 64, 128), f32),
        ]
        + [pltpu.VMEM(value.shape, value.dtype) for value in operands[1:]]
        + [
            pltpu.VMEM((8, 2, 3, 64, 128), f32),
            pltpu.VMEM((128, 4), f32),
            pltpu.VMEM((8, 128, 384), f32),
            pltpu.VMEM((16, 64, 384), f32),
            pltpu.VMEM((1152, 768), f32),
            pltpu.VMEM((384, 768), f32),
            pltpu.VMEM((16, 24, 768), f32),
            pltpu.VMEM((2, 384, 1024), jnp.bfloat16),
            pltpu.VMEM((2, 384, 1024), jnp.bfloat16),
            pltpu.VMEM((2, 144, 1024), f32),
            pltpu.VMEM((120, 256), f32),
            pltpu.VMEM((4, 72, 256), f32),
            pltpu.VMEM((4, 48, 256), f32),
            pltpu.VMEM((2, 120, 1024), f32),
            pltpu.VMEM((2, 72, 1024), f32),
            pltpu.VMEM((16, 120, 128), f32),
            pltpu.VMEM((16, 120, 128), f32),
            pltpu.VMEM((16, 72, 128), f32),
            pltpu.VMEM((16, 72, 128), f32),
            pltpu.SemaphoreType.DMA((8,)),
            pltpu.SemaphoreType.DMA((8,)),
            pltpu.SemaphoreType.DMA((8,)),
            pltpu.SemaphoreType.DMA((2,)),
            pltpu.SemaphoreType.DMA((2,)),
        ]
        + [pltpu.SemaphoreType.DMA((16,))] * 8,
        compiler_params=pltpu.CompilerParams(
            collective_id=0, has_side_effects=True, vmem_limit_bytes=56 * 2**20
        ),
    )(*operands)


def solution(mesh):
    placed = (
        P(None, None, "plane", "elem"),
        P(None, "elem"),
        P("elem", None),
        P("elem", None),
        P("elem", None),
    )
    return jax.shard_map(
        shards,
        mesh=mesh,
        in_specs=placed,
        out_specs=P(None, None, "plane", "elem"),
        check_vma=False,
    )
```

```python
import jax
import jax.numpy as jnp
import ml_dtypes
import numpy as np
from jax import lax
from jax.experimental import pallas as pl
from jax.experimental.pallas import tpu as pltpu
from jax.sharding import PartitionSpec as P

PLANES = 1024
POINTS = 64
LEADER, CLERK = 2, 3
MESH = pl.DeviceIdType.MESH
highest = lax.Precision.HIGHEST
gll_nodes = [
    -1.0,
    -0.8717401485096066,
    -0.5917001814331423,
    -0.2092992179024789,
    0.2092992179024789,
    0.5917001814331423,
    0.8717401485096066,
    1.0,
]


def legendre_seven(point_value):
    earlier_value = 1.0
    current_value = point_value
    for degree_index in range(1, 7):
        next_value = (
            (2 * degree_index + 1) * point_value * current_value - degree_index * earlier_value
        ) / (degree_index + 1)
        earlier_value = current_value
        current_value = next_value
    return current_value


def gll_matrices():
    legendre_vals = [legendre_seven(node_value) for node_value in gll_nodes]
    deriv_matrix = np.zeros((8, 8))
    for row_index in range(8):
        for col_index in range(8):
            if row_index != col_index:
                deriv_matrix[row_index, col_index] = (
                    legendre_vals[row_index]
                    / legendre_vals[col_index]
                    / (gll_nodes[row_index] - gll_nodes[col_index])
                )
    deriv_matrix[0, 0] = -14.0
    deriv_matrix[7, 7] = 14.0
    identity = np.eye(8)
    return (np.kron(identity, deriv_matrix), np.kron(deriv_matrix, identity))


def halves(matrix):
    high = matrix.astype(ml_dtypes.bfloat16)
    low = (matrix - high.astype(np.float64)).astype(ml_dtypes.bfloat16)
    return high, low


def point_order():
    steps = range(1, 7)
    order = [p for p in steps] + [8 * p + 7 for p in steps]
    order += [56 + p for p in steps] + [8 * p for p in steps]
    return order + [r for r in range(POINTS) if r not in order]


def tables():
    order = point_order()
    xi, eta = gll_matrices()
    eye = np.eye(POINTS)[order]
    pair = np.kron(np.eye(2), eye)
    edge_xi = np.kron(np.eye(2), xi[order[:24]])
    edge_eta = np.kron(np.eye(2), eta[order[:24]])
    pack_high, pack_low = halves(np.concatenate([pair, edge_xi, edge_eta]))
    pack = np.concatenate([pack_high, pack_low[128:]])

    k = (64 * np.arange(8)[:, None] + np.arange(64)[None, :])[:, None, :]
    waves = []
    for block in range(4):
        plane = 2 * (256 * (block % 2) + np.arange(256)) + block // 2
        angle = (k[..., None] * plane) % PLANES * (2.0 * np.pi / PLANES)
        waves.append(np.concatenate([np.cos(angle), -np.sin(angle)], axis=1).reshape(1024, 256))
    wave = np.stack(halves(np.stack(waves)))

    mode = 64 * np.arange(16)[:, None] + np.arange(64)[None, :]
    factor = 2.0 * np.where(mode < 512, mode, mode - 1024)
    dense = np.zeros((144, 128), np.float32)
    dense[:64, :64] = xi[order][:, order]
    dense[64:128, :64] = eta[order][:, order]
    dense[128:] = np.concatenate([-factor, factor], axis=1)

    def unpack(points):
        out = np.zeros((2, 3, len(points), 3, 128))
        for side in range(2):
            for field in range(3):
                for r, point in enumerate(points):
                    out[side, field, r, field, 64 * side + point] = 1.0
        return out.reshape(6 * len(points), 384).astype(ml_dtypes.bfloat16)

    turn = np.concatenate([unpack(order[:24]), unpack(order[24:])])
    return pack, dense, turn, wave


def split(x):
    high = x.astype(jnp.bfloat16)
    return high, (x - high.astype(jnp.float32)).astype(jnp.bfloat16)


def mm(a, b, dims=((1,), (0,))):
    return lax.dot_general(a, b, (dims, ((), ())), preferred_element_type=jnp.float32)


NT = ((1,), (1,))
TN = ((0,), (0,))


def mm3(a, b, dims=((1,), (0,))):
    return mm(a[0], b[0], dims) + (mm(a[0], b[1], dims) + mm(a[1], b[0], dims))


def exact(a, b, dims=((1,), (0,))):
    return lax.dot_general(
        a, b, (dims, ((), ())), precision=highest, preferred_element_type=jnp.float32
    )


def kernel(
    modes_hbm, geometry_hbm, neighbour_hbm, neighbour_edge_hbm, flipped_hbm,
    pack_hbm, dense_hbm, turn_hbm, wave_hbm,
    out_hbm,
    modes, geometry, neighbour, neighbour_edge, flipped, pack_table, dense, turn_table, wave, out,
    geo_column, send_vel, recv_vel, traces, far, recv_far, left_high, left_low,
    left_edge, rest, own_edge, uv_edge, total_rest, total_edge, send_rest, recv_rest, send_edge, recv_edge,
    plane_ok, elem_ok, load_sem, mode_sem, out_sem,
    trace_send, trace_recv, vel_s, vel_r, far_s, far_r, rest_s, rest_r, edge_s, edge_r,
):
    me = lax.axis_index("plane")
    group = lax.axis_index("elem")
    z = me // 2
    x = me % 2

    def peer(i):
        h = i // 2
        dz = (h + 1) // 2 * (2 * (h % 2) - 1)
        return (z + dz + 8) % 8 * 2 + (x + i) % 2

    barrier = pltpu.get_barrier_semaphore()
    before = (group + 15) % 16
    after = (group + 1) % 16

    def greet(i, carry):
        @pl.when(peer(i) != CLERK)
        def _():
            pl.semaphore_signal(barrier, inc=1, device_id={"plane": peer(i)}, device_id_type=MESH)

        return carry

    lax.fori_loop(1, 16, greet, 0)
    for other in (before, after):
        pl.semaphore_signal(
            barrier, inc=1, device_id={"plane": CLERK, "elem": other}, device_id_type=MESH
        )

    def enter_plane():
        @pl.when(me != CLERK)
        def _():
            pl.semaphore_wait(barrier, 15)

        @pl.when(me == LEADER)
        def _():
            pl.semaphore_signal(plane_ok, inc=1, device_id={"plane": CLERK}, device_id_type=MESH)

        @pl.when(me == CLERK)
        def _():
            pl.semaphore_wait(plane_ok, 1)

    def enter_elem():
        @pl.when(me == CLERK)
        def _():
            pl.semaphore_wait(barrier, 32)

            def tell(i, carry):
                pl.semaphore_signal(
                    elem_ok, inc=1, device_id={"plane": peer(i)}, device_id_type=MESH
                )
                return carry

            lax.fori_loop(1, 16, tell, 0)

        @pl.when(me != CLERK)
        def _():
            pl.semaphore_wait(elem_ok, 1)

    def pair_cols(q):
        return pl.ds(pl.multiple_of(128 * q, 128), 128)

    def mode_load(q):
        return pltpu.make_async_copy(modes_hbm.at[:, :, :, pair_cols(q)], modes.at[q], mode_sem.at[q])

    loads = [
        pltpu.make_async_copy(source, target, load_sem.at[i])
        for i, (source, target) in enumerate((
            (pack_hbm, pack_table),
            (geometry_hbm, geometry),
            (neighbour_hbm, neighbour),
            (neighbour_edge_hbm, neighbour_edge),
            (flipped_hbm, flipped),
            (dense_hbm, dense),
            (wave_hbm, wave),
            (turn_hbm, turn_table),
        ))
    ]
    loads[0].start()
    mode_load(peer(2) // 2).start()
    loads[1].start()

    def mode_start(h, carry):
        mode_load(peer(2 * h) // 2).start()
        return carry

    lax.fori_loop(2, 8, mode_start, 0)
    mode_load(z).start()
    for load in loads[2:]:
        load.start()

    def pack(q):
        mode_load(q).wait()
        block = jnp.concatenate([modes[q, c, f] for f in range(3) for c in range(2)], axis=0)
        high, low = split(block)
        both = mm(pack_table[:224], high, NT) + mm(pack_table[:224], low, NT)
        send_vel[q] = both[:128]
        along = both[128:] + mm(pack_table[224:], high, NT)
        pick = jnp.concatenate([pack_table[:24], pack_table[64:88]], axis=0).astype(jnp.float32)
        geo = exact(pick, geometry[:, pair_cols(q)], NT)
        rows = pl.ds(pl.multiple_of(48 * q, 16), 48)
        traces[rows, :384] = geo[:, 0:1] * along[:48] + geo[:, 1:2] * along[48:]
        traces[rows, 384:] = geo[:, 2:3] * along[:48] + geo[:, 3:4] * along[48:]

    def vel_part(p):
        return send_vel.at[p // 2, pl.ds(pl.multiple_of(p % 2 * 64, 64), 64)]

    def vel_copy(p, slot):
        return pltpu.make_async_remote_copy(
            vel_part(p), recv_vel.at[slot], vel_s.at[p], vel_r.at[slot],
            device_id={"plane": p}, device_id_type=MESH,
        )

    loads[0].wait()
    loads[1].wait()
    pack(peer(2) // 2)
    enter_plane()
    vel_copy(peer(2), me).start()
    vel_copy(peer(3), me).start()

    def pack_step(h, carry):
        pack(peer(2 * h) // 2)
        vel_copy(peer(2 * h), me).start()
        vel_copy(peer(2 * h + 1), me).start()
        return carry

    lax.fori_loop(2, 8, pack_step, 0)
    pack(z)
    vel_copy(peer(1), me).start()
    recv_vel[me] = send_vel[z, pl.ds(pl.multiple_of(x * 64, 64), 64), :]

    enter_elem()

    def trace_copy(slot, other):
        return pltpu.make_async_remote_copy(
            traces.at[pl.ds(0, 384)], traces.at[pl.ds(384 * (slot + 1), 384)],
            trace_send.at[slot], trace_recv.at[slot],
            device_id={"elem": other}, device_id_type=MESH,
        )

    trace_copies = [trace_copy(0, after), trace_copy(1, before)]
    for copy in trace_copies:
        copy.start()

    for load in loads[2:6]:
        load.wait()

    def iota(shape, axis):
        return lax.broadcasted_iota(jnp.int32, shape, axis)

    def rows_of(shape):
        row = iota(shape, 0)
        element = (row * 2731) >> 16
        edge = ((row - element * 24) * 10923) >> 16
        return element, edge, row - element * 24 - edge * 6

    near = jnp.maximum(neighbour[...], 0)
    offset = ((near >> 4) - group + 16) & 15
    where = jnp.where(offset == 0, 0, jnp.where(offset == 1, 2, 1))
    start = where * 384 + (near & 15) * 24 + neighbour_edge[...] * 6 + flipped[...] * 5
    start = jnp.where(neighbour[...] >= 0, start, -5000).astype(jnp.float32)
    turn = (1 - 2 * flipped[...]).astype(jnp.float32)
    owner = (rows_of((384, 16))[0] == iota((384, 16), 1)).astype(jnp.float32)
    edge = (rows_of((384, 4))[1] == iota((384, 4), 1)).astype(jnp.float32)
    place = rows_of((384, 1))[2].astype(jnp.float32)
    start = jnp.sum(exact(owner, start, NT) * edge, axis=1, keepdims=True)
    turn = jnp.sum(exact(owner, turn, NT) * edge, axis=1, keepdims=True)
    target = start + turn * place
    pick = jnp.where(iota((384, 1152), 1).astype(jnp.float32) == target, 0.5, 0.0)
    pick = pick.astype(jnp.bfloat16)

    geo_column[...] = exact(pack_table[:128].astype(jnp.float32), geometry[:, pair_cols(z)], NT)
    geo = geo_column[pl.ds(pl.multiple_of(64 * x, 64), 64), :]
    joined = jnp.where(neighbour[...] >= 0, 0.5, 0.0)
    edge_own = (rows_of((64, 4))[1] + 4 * rows_of((64, 4))[0] == iota((64, 4), 1))
    joined = exact(edge_own.astype(jnp.float32), joined)
    joined = jnp.where(iota((64, 16), 1) == me, joined, 0.0)
    keep = 1.0 - jnp.sum(joined, axis=1, keepdims=True)
    own_xi, own_eta = dense[:64, :64], dense[64:128, :64]
    to_x = keep * (geo[:, 0:1] * own_xi + geo[:, 1:2] * own_eta)
    to_y = keep * (geo[:, 2:3] * own_xi + geo[:, 3:4] * own_eta)
    gradient = split(jnp.concatenate([to_x, to_y], axis=0))

    for copy in trace_copies:
        copy.wait_recv()

    for j in range(3):
        high, low = split(traces[:, 256 * j : 256 * j + 256])
        far[:, 256 * j : 256 * j + 256] = mm(pick, high) + mm(pick, low)

    def far_part(p):
        return far.at[pl.ds(pl.multiple_of(24 * p, 8), 24)]

    def far_copy(p, slot):
        return pltpu.make_async_remote_copy(
            far_part(p), recv_far.at[slot], far_s.at[p], far_r.at[slot],
            device_id={"plane": p}, device_id_type=MESH,
        )

    def far_step(i, carry):
        far_copy(peer(i), me).start()
        return carry

    lax.fori_loop(1, 16, far_step, 0)
    recv_far[me] = far[pl.ds(pl.multiple_of(24 * me, 8), 24), :]

    def vel_wait(i, carry):
        vel_copy(peer(i), peer(i)).wait_recv()
        return carry

    lax.fori_loop(1, 16, vel_wait, 0)

    def gather(a, carry):
        lanes = pl.ds(pl.multiple_of(128 * a, 128), 128)
        for f in range(3):
            one = recv_vel[a, :, 128 * f : 128 * f + 128]
            two = recv_vel[a + 8, :, 128 * f : 128 * f + 128]
            one_z = pltpu.roll(one, 64, 1) * dense[pl.ds(128 + a, 1), :]
            two_z = pltpu.roll(two, 64, 1) * dense[pl.ds(136 + a, 1), :]
            for r, (p, q) in enumerate(((one, two), (one_z, two_z))):
                rows = slice(192 * r + 64 * f, 192 * r + 64 * f + 64)
                high, low = split(p + q)
                left_high[0, rows, lanes] = high
                left_low[0, rows, lanes] = low
                high, low = split(p - q)
                left_high[1, rows, lanes] = high
                left_low[1, rows, lanes] = low
        return carry

    lax.fori_loop(0, 8, gather, 0)
    for load in loads[6:]:
        load.wait()

    total_rest[...] = jnp.zeros_like(total_rest)
    total_edge[...] = jnp.zeros_like(total_edge)

    def planes(n, carry):
        parity = n // 2
        waves = (wave[0, n], wave[1, n])
        physical = mm3((left_high[parity], left_low[parity]), waves)
        u, v, w = physical[:64], physical[64:128], physical[128:192]
        uv_edge[n, :24] = u[:24]
        uv_edge[n, 24:] = v[:24]
        for f, field in enumerate((u, v, w)):
            slopes = mm3(gradient, split(field))
            spanwise = physical[192 + 64 * f : 256 + 64 * f]
            product = u * slopes[:64] + v * slopes[64:] + w * spanwise
            own_edge[n, 24 * f : 24 * f + 24] = product[:24]
            rest[40 * f : 40 * f + 40] = product[24:]
        total_rest[parity] += mm3(split(rest[...]), waves, NT)
        return carry

    lax.fori_loop(0, 4, planes, 0)

    def combine(total, send):
        for a in range(8):
            even = total[0, :, 128 * a : 128 * a + 128]
            odd = total[1, :, 128 * a : 128 * a + 128]
            send[a] = (even + odd) * (1.0 / PLANES)
            send[a + 8] = (even - odd) * (1.0 / PLANES)

    def back_copy(send, recv, send_sem, recv_sem, p, slot):
        return pltpu.make_async_remote_copy(
            send.at[p], recv.at[slot], send_sem.at[p], recv_sem.at[slot],
            device_id={"plane": p}, device_id_type=MESH,
        )

    def back(total, send, recv, send_sem, recv_sem):
        combine(total, send)

        def step(i, carry):
            back_copy(send, recv, send_sem, recv_sem, peer(i), me).start()
            return carry

        lax.fori_loop(1, 16, step, 0)
        recv[me] = send[me]

    back(total_rest, send_rest, recv_rest, rest_s, rest_r)

    def far_wait(i, carry):
        far_copy(peer(i), peer(i)).wait_recv()
        return carry

    lax.fori_loop(1, 16, far_wait, 0)

    def gather_far(a, carry):
        lanes = pl.ds(pl.multiple_of(128 * a, 128), 128)
        for g in range(6):
            one = recv_far[a, :, 128 * g : 128 * g + 128]
            two = recv_far[a + 8, :, 128 * g : 128 * g + 128]
            left_edge[0, 24 * g : 24 * g + 24, lanes] = one + two
            left_edge[1, 24 * g : 24 * g + 24, lanes] = one - two
        return carry

    lax.fori_loop(0, 8, gather_far, 0)

    def edges(n, carry):
        parity = n // 2
        waves = (wave[0, n], wave[1, n])
        slopes = mm3(split(left_edge[parity]), waves)
        u, v = uv_edge[n, :24], uv_edge[n, 24:]
        product = jnp.concatenate(
            [
                own_edge[n, 24 * f : 24 * f + 24]
                + u * slopes[24 * f : 24 * f + 24]
                + v * slopes[72 + 24 * f : 96 + 24 * f]
                for f in range(3)
            ],
            axis=0,
        )
        total_edge[parity] += mm3(split(product), waves, NT)
        return carry

    lax.fori_loop(0, 4, edges, 0)
    back(total_edge, send_edge, recv_edge, edge_s, edge_r)

    def out_copy(q):
        return pltpu.make_async_copy(out.at[q], out_hbm.at[:, :, :, pair_cols(q)], out_sem.at[q])

    def unpack(q, recv, rows, add):
        high, low = split(jnp.concatenate([recv[2 * q], recv[2 * q + 1]], axis=0))
        turned = mm(high, turn_table[rows], TN) + mm(low, turn_table[rows], TN)
        for c in range(2):
            for f in range(3):
                part = turned[64 * c : 64 * c + 64, 128 * f : 128 * f + 128]
                if add:
                    part = part + out[q, c, f]
                out[q, c, f] = part
        if add:
            out_copy(q).start()

    def unpack_all(send, recv, send_sem, recv_sem, rows, add):
        def arrive(i):
            back_copy(send, recv, send_sem, recv_sem, peer(i), peer(i)).wait_recv()

        def step(h, carry):
            arrive(2 * h)
            arrive(2 * h + 1)
            unpack(peer(2 * h) // 2, recv, rows, add)
            return carry

        arrive(1)
        unpack(z, recv, rows, add)
        lax.fori_loop(1, 8, step, 0)

    unpack_all(send_rest, recv_rest, rest_s, rest_r, slice(144, 384), False)
    unpack_all(send_edge, recv_edge, edge_s, edge_r, slice(0, 144), True)

    def drain(i, carry):
        p = peer(i)
        vel_copy(p, me).wait_send()
        far_copy(p, me).wait_send()
        back_copy(send_rest, recv_rest, rest_s, rest_r, p, me).wait_send()
        back_copy(send_edge, recv_edge, edge_s, edge_r, p, me).wait_send()
        return carry

    lax.fori_loop(1, 16, drain, 0)
    for copy in trace_copies:
        copy.wait_send()
    for q in range(8):
        out_copy(q).wait()


def shards(velocity_modes, geometry, neighbour, neighbour_edge, flipped):
    constants = [jnp.asarray(value) for value in tables()]
    anywhere = pl.BlockSpec(memory_space=pl.ANY)
    f32 = jnp.float32
    operands = (velocity_modes, geometry, neighbour.T, neighbour_edge.T, flipped.T, *constants)
    return pl.pallas_call(
        kernel,
        out_shape=jax.ShapeDtypeStruct(velocity_modes.shape, f32),
        in_specs=[anywhere] * len(operands),
        out_specs=anywhere,
        scratch_shapes=[
            pltpu.VMEM((8, 2, 3, 64, 128), f32),
        ]
        + [pltpu.VMEM(value.shape, value.dtype) for value in operands[1:]]
        + [
            pltpu.VMEM((8, 2, 3, 64, 128), f32),
            pltpu.VMEM((128, 4), f32),
            pltpu.VMEM((8, 128, 384), f32),
            pltpu.VMEM((16, 64, 384), f32),
            pltpu.VMEM((1152, 768), f32),
            pltpu.VMEM((384, 768), f32),
            pltpu.VMEM((16, 24, 768), f32),
            pltpu.VMEM((2, 384, 1024), jnp.bfloat16),
            pltpu.VMEM((2, 384, 1024), jnp.bfloat16),
            pltpu.VMEM((2, 144, 1024), f32),
            pltpu.VMEM((120, 256), f32),
            pltpu.VMEM((4, 72, 256), f32),
            pltpu.VMEM((4, 48, 256), f32),
            pltpu.VMEM((2, 120, 1024), f32),
            pltpu.VMEM((2, 72, 1024), f32),
            pltpu.VMEM((16, 120, 128), f32),
            pltpu.VMEM((16, 120, 128), f32),
            pltpu.VMEM((16, 72, 128), f32),
            pltpu.VMEM((16, 72, 128), f32),
            pltpu.SemaphoreType.REGULAR,
            pltpu.SemaphoreType.REGULAR,
            pltpu.SemaphoreType.DMA((8,)),
            pltpu.SemaphoreType.DMA((8,)),
            pltpu.SemaphoreType.DMA((8,)),
            pltpu.SemaphoreType.DMA((2,)),
            pltpu.SemaphoreType.DMA((2,)),
        ]
        + [pltpu.SemaphoreType.DMA((16,))] * 8,
        compiler_params=pltpu.CompilerParams(
            collective_id=0, has_side_effects=True, vmem_limit_bytes=56 * 2**20
        ),
    )(*operands)


def solution(mesh):
    placed = (
        P(None, None, "plane", "elem"),
        P(None, "elem"),
        P("elem", None),
        P("elem", None),
        P("elem", None),
    )
    return jax.shard_map(
        shards,
        mesh=mesh,
        in_specs=placed,
        out_specs=P(None, None, "plane", "elem"),
        check_vma=False,
    )
```

```python
import jax
import jax.numpy as jnp
import ml_dtypes
import numpy as np
from jax import lax
from jax.experimental import pallas as pl
from jax.experimental.pallas import tpu as pltpu
from jax.sharding import PartitionSpec as P

PLANES = 1024
POINTS = 64
LEADER, CLERK = 2, 3
EARLY, MIDDLE = 16, 12
FIRST = 64
MESH = pl.DeviceIdType.MESH
highest = lax.Precision.HIGHEST
gll_nodes = [
    -1.0,
    -0.8717401485096066,
    -0.5917001814331423,
    -0.2092992179024789,
    0.2092992179024789,
    0.5917001814331423,
    0.8717401485096066,
    1.0,
]


def legendre_seven(point_value):
    earlier_value = 1.0
    current_value = point_value
    for degree_index in range(1, 7):
        next_value = (
            (2 * degree_index + 1) * point_value * current_value - degree_index * earlier_value
        ) / (degree_index + 1)
        earlier_value = current_value
        current_value = next_value
    return current_value


def gll_matrices():
    legendre_vals = [legendre_seven(node_value) for node_value in gll_nodes]
    deriv_matrix = np.zeros((8, 8))
    for row_index in range(8):
        for col_index in range(8):
            if row_index != col_index:
                deriv_matrix[row_index, col_index] = (
                    legendre_vals[row_index]
                    / legendre_vals[col_index]
                    / (gll_nodes[row_index] - gll_nodes[col_index])
                )
    deriv_matrix[0, 0] = -14.0
    deriv_matrix[7, 7] = 14.0
    identity = np.eye(8)
    return (np.kron(identity, deriv_matrix), np.kron(deriv_matrix, identity))


def halves(matrix):
    high = matrix.astype(ml_dtypes.bfloat16)
    low = (matrix - high.astype(np.float64)).astype(ml_dtypes.bfloat16)
    return high, low


def point_order():
    steps = range(1, 7)
    order = [p for p in steps] + [8 * p + 7 for p in steps]
    order += [56 + p for p in steps] + [8 * p for p in steps]
    return order + [r for r in range(POINTS) if r not in order]


def tables():
    order = point_order()
    xi, eta = gll_matrices()
    pair = np.kron(np.eye(2), np.eye(POINTS)[order]).astype(ml_dtypes.bfloat16)

    k = (64 * np.arange(8)[:, None] + np.arange(64)[None, :])[:, None, :]
    waves = []
    for block in range(4):
        plane = 2 * (256 * (block % 2) + np.arange(256)) + block // 2
        angle = (k[..., None] * plane) % PLANES * (2.0 * np.pi / PLANES)
        waves.append(np.concatenate([np.cos(angle), -np.sin(angle)], axis=1).reshape(1024, 256))
    wave = np.stack(halves(np.stack(waves)))

    mode = 64 * np.arange(16)[:, None] + np.arange(64)[None, :]
    factor = 2.0 * np.where(mode < 512, mode, mode - 1024)
    dense = np.zeros((144, 128), np.float32)
    dense[:64, :64] = xi[order][:, order]
    dense[64:128, :64] = eta[order][:, order]
    dense[128:] = np.concatenate([-factor, factor], axis=1)
    return pair, dense, wave, np.ascontiguousarray(wave.transpose(0, 1, 3, 2))


def split(x):
    high = x.astype(jnp.bfloat16)
    return high, (x - high.astype(jnp.float32)).astype(jnp.bfloat16)


def mm(a, b, dims=((1,), (0,))):
    return lax.dot_general(a, b, (dims, ((), ())), preferred_element_type=jnp.float32)


NT = ((1,), (1,))
TN = ((0,), (0,))


def mm3(a, b, dims=((1,), (0,))):
    return mm(a[0], b[0], dims) + (mm(a[0], b[1], dims) + mm(a[1], b[0], dims))


def exact(a, b, dims=((1,), (0,))):
    return lax.dot_general(
        a, b, (dims, ((), ())), precision=highest, preferred_element_type=jnp.float32
    )


def kernel(
    modes_hbm, geometry_hbm, neighbour_hbm, neighbour_edge_hbm, flipped_hbm,
    pair_hbm, dense_hbm, wave_hbm, back_wave_hbm,
    out_hbm,
    modes, geometry, neighbour, neighbour_edge, flipped, pair, dense, wave, back_wave, out,
    geo_column, send_vel, recv_vel, traces, far, recv_far, left_high, left_low, physical,
    left_far, far_modes, slopes_edge, product, total, total_far, send_main, recv_main, send_far, shares, added,
    plane_ok, elem_ok, load_sem, mode_sem, out_sem,
    trace_send, trace_recv, share_send, share_recv, vel_s, vel_r, far_s, far_r, main_s, main_r, back_s, back_r,
):
    me = lax.axis_index("plane")
    group = lax.axis_index("elem")
    z = me // 2
    x = me % 2

    def peer(i):
        h = i // 2
        dz = (h + 1) // 2 * (2 * (h % 2) - 1)
        return (z + dz + 8) % 8 * 2 + (x + i) % 2

    barrier = pltpu.get_barrier_semaphore()
    before = (group + 15) % 16
    after = (group + 1) % 16

    def greet(i, carry):
        @pl.when(peer(i) != CLERK)
        def _():
            pl.semaphore_signal(barrier, inc=1, device_id={"plane": peer(i)}, device_id_type=MESH)

        return carry

    lax.fori_loop(1, 16, greet, 0)
    for other in (before, after):
        pl.semaphore_signal(
            barrier, inc=1, device_id={"plane": CLERK, "elem": other}, device_id_type=MESH
        )

    def enter_plane():
        @pl.when(me != CLERK)
        def _():
            pl.semaphore_wait(barrier, 15)

        @pl.when(me == LEADER)
        def _():
            pl.semaphore_signal(plane_ok, inc=1, device_id={"plane": CLERK}, device_id_type=MESH)

        @pl.when(me == CLERK)
        def _():
            pl.semaphore_wait(plane_ok, 1)

    def enter_elem():
        @pl.when(me == CLERK)
        def _():
            pl.semaphore_wait(barrier, 32)

            def tell(i, carry):
                pl.semaphore_signal(
                    elem_ok, inc=1, device_id={"plane": peer(i)}, device_id_type=MESH
                )
                return carry

            lax.fori_loop(1, 16, tell, 0)

        @pl.when(me != CLERK)
        def _():
            pl.semaphore_wait(elem_ok, 1)

    def pair_cols(q):
        return pl.ds(pl.multiple_of(128 * q, 128), 128)

    def mode_load(q):
        return pltpu.make_async_copy(modes_hbm.at[:, :, :, pair_cols(q)], modes.at[q], mode_sem.at[q])

    loads = [
        pltpu.make_async_copy(source, target, load_sem.at[i])
        for i, (source, target) in enumerate((
            (pair_hbm, pair),
            (geometry_hbm, geometry),
            (neighbour_hbm, neighbour),
            (neighbour_edge_hbm, neighbour_edge),
            (flipped_hbm, flipped),
            (dense_hbm, dense),
            (wave_hbm, wave),
            (back_wave_hbm, back_wave),
        ))
    ]
    loads[0].start()
    mode_load(peer(2) // 2).start()
    loads[1].start()

    def mode_start(h, carry):
        mode_load(peer(2 * h) // 2).start()
        return carry

    lax.fori_loop(2, 8, mode_start, 0)
    mode_load(z).start()
    for load in loads[2:]:
        load.start()

    def pack(q):
        mode_load(q).wait()
        block = jnp.concatenate([modes[q, c, f] for f in range(3) for c in range(2)], axis=0)
        high, low = split(block)
        send_vel[q] = mm(pair[...], high, NT) + mm(pair[...], low, NT)

    def vel_part(p):
        return send_vel.at[p // 2, pl.ds(pl.multiple_of(p % 2 * 64, 64), 64)]

    def vel_copy(p, slot):
        return pltpu.make_async_remote_copy(
            vel_part(p), recv_vel.at[slot], vel_s.at[p], vel_r.at[slot],
            device_id={"plane": p}, device_id_type=MESH,
        )

    loads[0].wait()
    pack(peer(2) // 2)
    enter_plane()
    vel_copy(peer(2), me).start()
    vel_copy(peer(3), me).start()

    def pack_step(h, carry):
        pack(peer(2 * h) // 2)
        vel_copy(peer(2 * h), me).start()
        vel_copy(peer(2 * h + 1), me).start()
        return carry

    lax.fori_loop(2, 8, pack_step, 0)
    pack(z)
    vel_copy(peer(1), me).start()
    recv_vel[me] = send_vel[z, pl.ds(pl.multiple_of(x * 64, 64), 64), :]

    for load in loads[1:6]:
        load.wait()

    def iota(shape, axis):
        return lax.broadcasted_iota(jnp.int32, shape, axis)

    def rows_of(shape):
        row = iota(shape, 0)
        element = (row * 2731) >> 16
        edge = ((row - element * 24) * 10923) >> 16
        return element, edge, row - element * 24 - edge * 6

    owner = (rows_of((384, 16))[0] == iota((384, 16), 1)).astype(jnp.float32)
    edge = (rows_of((384, 4))[1] == iota((384, 4), 1)).astype(jnp.float32)

    def per_row(table):
        return jnp.sum(exact(owner, table, NT) * edge, axis=1, keepdims=True)

    def one_hot(width, target):
        return iota((384, width), 1).astype(jnp.float32) == target

    near = jnp.maximum(neighbour[...], 0)
    offset = ((near >> 4) - group + 16) & 15
    where = jnp.where(offset == 0, 0, jnp.where(offset == 1, 2, 1))
    start = where * 384 + (near & 15) * 24 + neighbour_edge[...] * 6
    start = per_row(jnp.where(neighbour[...] >= 0, start, -5000).astype(jnp.float32))
    place = rows_of((384, 1))[2].astype(jnp.float32)
    turned = per_row(flipped[...].astype(jnp.float32))
    turned = place + turned * (5.0 - 2.0 * place)
    row = iota((384, 1), 0).astype(jnp.float32)
    turn = jnp.where(one_hot(384, row - place + turned), 1.0, 0.0).astype(jnp.bfloat16)

    for e in range(16):
        left_far[24 * e : 24 * e + 24] = send_vel[e // 2, 64 * (e % 2) : 64 * (e % 2) + 24, :256]
    high, low = split(left_far[...])
    traces[:384] = mm(turn, high) + mm(turn, low)

    enter_elem()

    def swap(array, width, send_sem, recv_sem):
        copies = [
            pltpu.make_async_remote_copy(
                array.at[pl.ds(0, 384)], array.at[pl.ds(384 * (slot + 1), 384)],
                send_sem.at[slot], recv_sem.at[slot],
                device_id={"elem": other}, device_id_type=MESH,
            )
            for slot, other in ((0, after), (1, before))
        ]
        for copy in copies:
            copy.start()
        return copies

    trace_copies = swap(traces, 256, trace_send, trace_recv)
    pick = jnp.where(one_hot(1152, start + place), 1.0, 0.0).astype(jnp.bfloat16)

    geo_column[...] = exact(pair[...].astype(jnp.float32), geometry[:, pair_cols(z)], NT)
    geo = geo_column[pl.ds(pl.multiple_of(64 * x, 64), 64), :]
    joined = jnp.where(neighbour[...] >= 0, 0.5, 0.0)
    edge_own = rows_of((64, 4))[1] + 4 * rows_of((64, 4))[0] == iota((64, 4), 1)
    joined = exact(edge_own.astype(jnp.float32), joined)
    joined = jnp.where(iota((64, 16), 1) == me, joined, 0.0)
    keep = 1.0 - jnp.sum(joined, axis=1, keepdims=True)
    own_xi, own_eta = dense[:64, :64], dense[64:128, :64]
    to_x = geo[:, 0:1] * own_xi + geo[:, 1:2] * own_eta
    to_y = geo[:, 2:3] * own_xi + geo[:, 3:4] * own_eta
    gradient = split(jnp.concatenate([to_x, to_y], axis=0))

    for copy in trace_copies:
        copy.wait_recv()
    high, low = split(traces[...])
    far[...] = mm(pick, high) + mm(pick, low)

    def far_part(p):
        return far.at[pl.ds(pl.multiple_of(24 * p, 8), 24)]

    def far_copy(p, slot):
        return pltpu.make_async_remote_copy(
            far_part(p), recv_far.at[slot], far_s.at[p], far_r.at[slot],
            device_id={"plane": p}, device_id_type=MESH,
        )

    def loop(low, high, body):
        def step(i, carry):
            body(i)
            return carry

        lax.fori_loop(low, high, step, 0)

    loop(2, EARLY, lambda i: vel_copy(peer(i), me).wait_send())
    loop(1, 16, lambda i: far_copy(peer(i), me).start())
    recv_far[me] = far[pl.ds(pl.multiple_of(24 * me, 8), 24), :]

    for load in loads[6:]:
        load.wait()

    for step, (dz, sources) in enumerate(
        ((1, (2, 3, 12, 13)), (3, (4, 5, 10, 11)), (2, (6, 7, 8, 9)), (0, (14, 15, 1)))
    ):
        for i in sources:
            vel_copy(peer(i), peer(i)).wait_recv()
        part = (z + dz) % 4

        for side in range(2):
            lanes = slice(128 * side, 128 * side + 128)
            a = 2 * part + side
            for f in range(3):
                one = recv_vel[a, :, 128 * f : 128 * f + 128]
                two = recv_vel[a + 8, :, 128 * f : 128 * f + 128]
                one_z = pltpu.roll(one, 64, 1) * dense[pl.ds(128 + a, 1), :]
                two_z = pltpu.roll(two, 64, 1) * dense[pl.ds(136 + a, 1), :]
                for r, (p, q) in enumerate(((one, two), (one_z, two_z))):
                    rows = slice(192 * r + 64 * f, 192 * r + 64 * f + 64)
                    high, low = split(p + q)
                    left_high[0, rows, lanes] = high
                    left_low[0, rows, lanes] = low
                    high, low = split(p - q)
                    left_high[1, rows, lanes] = high
                    left_low[1, rows, lanes] = low

        def inverse(n, first=step == 0, part=part):
            rows = pl.ds(pl.multiple_of(256 * part, 256), 256)
            waves = (wave[0, n, rows, :], wave[1, n, rows, :])
            term = mm3((left_high[n // 2], left_low[n // 2]), waves)
            physical[n] = term if first else physical[n] + term

        loop(0, 4, inverse)

    total[...] = jnp.zeros_like(total)
    total_far[...] = jnp.zeros_like(total_far)

    def advect(n):
        u, v, w = (physical[n, 64 * f : 64 * f + 64] for f in range(3))
        for f, field in enumerate((u, v, w)):
            slopes = mm3(gradient, split(field))
            slopes_edge[n, 24 * f : 24 * f + 24] = slopes[:24]
            slopes_edge[n, 72 + 24 * f : 96 + 24 * f] = slopes[64:88]
            spanwise = physical[n, 192 + 64 * f : 256 + 64 * f]
            product[64 * f : 64 * f + 64] = (
                keep * (u * slopes[:64] + v * slopes[64:]) + w * spanwise
            )
        total[n // 2] += mm3(split(product[...]), (back_wave[0, n], back_wave[1, n]))

    loop(0, 4, advect)

    def both(sums, rows, a):
        lanes = slice(128 * a, 128 * a + 128)
        even, odd = sums[0, rows, lanes], sums[1, rows, lanes]
        return (even + odd) * (1.0 / PLANES), (even - odd) * (1.0 / PLANES)

    def main_copy(part, p, slot):
        rows = pl.ds(*((0, FIRST), (FIRST, 192 - FIRST))[part])
        return pltpu.make_async_remote_copy(
            send_main.at[p, rows], recv_main.at[slot, rows],
            main_s.at[part, p], main_r.at[part, slot],
            device_id={"plane": p}, device_id_type=MESH,
        )

    def send_part(part):
        rows = slice(*((0, FIRST), (FIRST, 192))[part])
        for a in range(8):
            send_main[a, rows], send_main[a + 8, rows] = both(total, rows, a)
        loop(1, 16, lambda i: main_copy(part, peer(i), me).start())
        recv_main[me, rows] = send_main[me, rows]

    send_part(0)

    loop(1, 16, lambda i: far_copy(peer(i), peer(i)).wait_recv())
    for a in range(8):
        lanes = slice(128 * a, 128 * a + 128)
        for f in range(2):
            one = recv_far[a, :, 128 * f : 128 * f + 128]
            two = recv_far[a + 8, :, 128 * f : 128 * f + 128]
            rows = slice(24 * f, 24 * f + 24)
            far_modes[0, rows, lanes] = one + two
            far_modes[1, rows, lanes] = one - two

    def advect_far(n):
        velocity = mm3(split(far_modes[n // 2]), (wave[0, n], wave[1, n]))
        u, v = velocity[:24], velocity[24:]
        terms = jnp.concatenate(
            [
                u * slopes_edge[n, 24 * f : 24 * f + 24]
                + v * slopes_edge[n, 72 + 24 * f : 96 + 24 * f]
                for f in range(3)
            ],
            axis=0,
        )
        total_far[n // 2] += mm3(split(terms), (back_wave[0, n], back_wave[1, n]))

    loop(0, 4, advect_far)

    def back_copy(p, slot):
        return pltpu.make_async_remote_copy(
            send_far.at[p], shares.at[pl.ds(pl.multiple_of(24 * slot, 8), 24)],
            back_s.at[p], back_r.at[slot],
            device_id={"plane": p}, device_id_type=MESH,
        )

    for a in range(8):
        for f in range(3):
            lanes = slice(128 * f, 128 * f + 128)
            plus, minus = both(total_far, slice(24 * f, 24 * f + 24), a)
            send_far[a, :, lanes] = plus
            send_far[a + 8, :, lanes] = minus
    loop(1, 16, lambda i: back_copy(peer(i), me).start())
    shares[pl.ds(pl.multiple_of(24 * me, 8), 24), :] = send_far[me]

    loop(2, MIDDLE, lambda i: back_copy(peer(i), me).wait_send())
    send_part(1)

    loop(1, 16, lambda i: back_copy(peer(i), peer(i)).wait_recv())
    share_copies = swap(shares, 384, share_send, share_recv)
    give = jnp.where(one_hot(1152, start + turned), 0.5, 0.0).astype(jnp.bfloat16)

    for copy in share_copies:
        copy.wait_recv()
    high, low = split(shares[...])
    added[...] = mm(give, high) + mm(give, low)

    def out_copy(q):
        return pltpu.make_async_copy(out.at[q], out_hbm.at[:, :, :, pair_cols(q)], out_sem.at[q])

    def unpack(q):
        rows = pl.ds(pl.multiple_of(48 * q, 16), 48)
        for f in range(3):
            extra = added[rows, 128 * f : 128 * f + 128]
            sides = []
            for side in range(2):
                one = recv_main[2 * q + side, 64 * f : 64 * f + 64]
                sides += [one[:24] + extra[24 * side : 24 * side + 24], one[24:]]
            high, low = split(jnp.concatenate(sides, axis=0))
            block = mm(high, pair[...], TN) + mm(low, pair[...], TN)
            out[q, 0, f] = block[:64]
            out[q, 1, f] = block[64:]
        out_copy(q).start()

    def arrive(i):
        for part in range(2):
            main_copy(part, peer(i), peer(i)).wait_recv()

    def unpack_step(h):
        arrive(2 * h)
        arrive(2 * h + 1)
        unpack(peer(2 * h) // 2)

    arrive(1)
    unpack(z)
    loop(1, 8, unpack_step)

    def drain(i):
        far_copy(peer(i), me).wait_send()
        for part in range(2):
            main_copy(part, peer(i), me).wait_send()

    loop(1, 16, drain)
    vel_copy(peer(1), me).wait_send()
    back_copy(peer(1), me).wait_send()
    loop(EARLY, 16, lambda i: vel_copy(peer(i), me).wait_send())
    loop(MIDDLE, 16, lambda i: back_copy(peer(i), me).wait_send())
    for copy in trace_copies + share_copies:
        copy.wait_send()
    for q in range(8):
        out_copy(q).wait()


def shards(velocity_modes, geometry, neighbour, neighbour_edge, flipped):
    constants = [jnp.asarray(value) for value in tables()]
    anywhere = pl.BlockSpec(memory_space=pl.ANY)
    f32 = jnp.float32
    operands = (velocity_modes, geometry, neighbour.T, neighbour_edge.T, flipped.T, *constants)
    return pl.pallas_call(
        kernel,
        out_shape=jax.ShapeDtypeStruct(velocity_modes.shape, f32),
        in_specs=[anywhere] * len(operands),
        out_specs=anywhere,
        scratch_shapes=[
            pltpu.VMEM((8, 2, 3, 64, 128), f32),
        ]
        + [pltpu.VMEM(value.shape, value.dtype) for value in operands[1:]]
        + [
            pltpu.VMEM((8, 2, 3, 64, 128), f32),
            pltpu.VMEM((128, 4), f32),
            pltpu.VMEM((8, 128, 384), f32),
            pltpu.VMEM((16, 64, 384), f32),
            pltpu.VMEM((1152, 256), f32),
            pltpu.VMEM((384, 256), f32),
            pltpu.VMEM((16, 24, 256), f32),
            pltpu.VMEM((2, 384, 256), jnp.bfloat16),
            pltpu.VMEM((2, 384, 256), jnp.bfloat16),
            pltpu.VMEM((4, 384, 256), f32),
            pltpu.VMEM((384, 256), f32),
            pltpu.VMEM((2, 48, 1024), f32),
            pltpu.VMEM((4, 144, 256), f32),
            pltpu.VMEM((192, 256), f32),
            pltpu.VMEM((2, 192, 1024), f32),
            pltpu.VMEM((2, 72, 1024), f32),
            pltpu.VMEM((16, 192, 128), f32),
            pltpu.VMEM((16, 192, 128), f32),
            pltpu.VMEM((16, 24, 384), f32),
            pltpu.VMEM((1152, 384), f32),
            pltpu.VMEM((384, 384), f32),
            pltpu.SemaphoreType.REGULAR,
            pltpu.SemaphoreType.REGULAR,
            pltpu.SemaphoreType.DMA((9,)),
            pltpu.SemaphoreType.DMA((8,)),
            pltpu.SemaphoreType.DMA((8,)),
        ]
        + [pltpu.SemaphoreType.DMA((2,))] * 4
        + [pltpu.SemaphoreType.DMA((16,))] * 4
        + [pltpu.SemaphoreType.DMA((2, 16))] * 2
        + [pltpu.SemaphoreType.DMA((16,))] * 2,
        compiler_params=pltpu.CompilerParams(
            collective_id=0, has_side_effects=True, vmem_limit_bytes=56 * 2**20
        ),
    )(*operands)


def solution(mesh):
    placed = (
        P(None, None, "plane", "elem"),
        P(None, "elem"),
        P("elem", None),
        P("elem", None),
        P("elem", None),
    )
    return jax.shard_map(
        shards,
        mesh=mesh,
        in_specs=placed,
        out_specs=P(None, None, "plane", "elem"),
        check_vma=False,
    )
```

```python
import jax
import jax.numpy as jnp
import ml_dtypes
import numpy as np
from jax import lax
from jax.experimental import pallas as pl
from jax.experimental.pallas import tpu as pltpu
from jax.sharding import PartitionSpec as P

PLANES = 1024
POINTS = 64
LEADER, CLERK = 2, 3
EARLY, MIDDLE = 16, 12
ARRIVALS = ((1, (2, 3, 12, 13)), (3, (4, 5, 10, 11)), (2, (6, 7, 8, 9)), (0, (14, 15, 1)))
FIRST = 64
MESH = pl.DeviceIdType.MESH
highest = lax.Precision.HIGHEST
gll_nodes = [
    -1.0,
    -0.8717401485096066,
    -0.5917001814331423,
    -0.2092992179024789,
    0.2092992179024789,
    0.5917001814331423,
    0.8717401485096066,
    1.0,
]


def legendre_seven(point_value):
    earlier_value = 1.0
    current_value = point_value
    for degree_index in range(1, 7):
        next_value = (
            (2 * degree_index + 1) * point_value * current_value - degree_index * earlier_value
        ) / (degree_index + 1)
        earlier_value = current_value
        current_value = next_value
    return current_value


def gll_matrices():
    legendre_vals = [legendre_seven(node_value) for node_value in gll_nodes]
    deriv_matrix = np.zeros((8, 8))
    for row_index in range(8):
        for col_index in range(8):
            if row_index != col_index:
                deriv_matrix[row_index, col_index] = (
                    legendre_vals[row_index]
                    / legendre_vals[col_index]
                    / (gll_nodes[row_index] - gll_nodes[col_index])
                )
    deriv_matrix[0, 0] = -14.0
    deriv_matrix[7, 7] = 14.0
    identity = np.eye(8)
    return (np.kron(identity, deriv_matrix), np.kron(deriv_matrix, identity))


def halves(matrix):
    high = matrix.astype(ml_dtypes.bfloat16)
    low = (matrix - high.astype(np.float64)).astype(ml_dtypes.bfloat16)
    return high, low


def point_order():
    steps = range(1, 7)
    order = [p for p in steps] + [8 * p + 7 for p in steps]
    order += [56 + p for p in steps] + [8 * p for p in steps]
    return order + [r for r in range(POINTS) if r not in order]


def tables():
    order = point_order()
    xi, eta = gll_matrices()
    pair = np.kron(np.eye(2), np.eye(POINTS)[order]).astype(ml_dtypes.bfloat16)

    k = (64 * np.arange(8)[:, None] + np.arange(64)[None, :])[:, None, :]
    waves = []
    for block in range(4):
        plane = 2 * (256 * (block % 2) + np.arange(256)) + block // 2
        angle = (k[..., None] * plane) % PLANES * (2.0 * np.pi / PLANES)
        waves.append(np.concatenate([np.cos(angle), -np.sin(angle)], axis=1).reshape(1024, 256))
    wave = np.stack(halves(np.stack(waves)))

    mode = 64 * np.arange(16)[:, None] + np.arange(64)[None, :]
    factor = 2.0 * np.where(mode < 512, mode, mode - 1024)
    dense = np.zeros((144, 128), np.float32)
    dense[:64, :64] = xi[order][:, order]
    dense[64:128, :64] = eta[order][:, order]
    dense[128:] = np.concatenate([-factor, factor], axis=1)
    return pair, dense, wave, np.ascontiguousarray(wave.transpose(0, 1, 3, 2))


def split(x):
    high = x.astype(jnp.bfloat16)
    return high, (x - high.astype(jnp.float32)).astype(jnp.bfloat16)


def mm(a, b, dims=((1,), (0,))):
    return lax.dot_general(a, b, (dims, ((), ())), preferred_element_type=jnp.float32)


NT = ((1,), (1,))
TN = ((0,), (0,))


def mm3(a, b, dims=((1,), (0,))):
    return mm(a[0], b[0], dims) + (mm(a[0], b[1], dims) + mm(a[1], b[0], dims))


def exact(a, b, dims=((1,), (0,))):
    return lax.dot_general(
        a, b, (dims, ((), ())), precision=highest, preferred_element_type=jnp.float32
    )


def kernel(
    modes_hbm, geometry_hbm, neighbour_hbm, neighbour_edge_hbm, flipped_hbm,
    pair_hbm, dense_hbm, wave_hbm, back_wave_hbm,
    out_hbm,
    modes, geometry, neighbour, neighbour_edge, flipped, pair, dense, wave, back_wave, out,
    geo_column, send_vel, recv_vel, traces, far, recv_far, left_high, left_low, physical,
    left_far, far_modes, far_physical, slopes_edge, product, total, total_far, send_main, recv_main, send_far, shares, added,
    plane_ok, elem_ok, load_sem, mode_sem, out_sem,
    trace_send, trace_recv, share_send, share_recv, vel_s, vel_r, far_s, far_r, main_s, main_r, back_s, back_r,
):
    me = lax.axis_index("plane")
    group = lax.axis_index("elem")
    z = me // 2
    x = me % 2

    def peer(i):
        h = i // 2
        dz = (h + 1) // 2 * (2 * (h % 2) - 1)
        return (z + dz + 8) % 8 * 2 + (x + i) % 2

    barrier = pltpu.get_barrier_semaphore()
    before = (group + 15) % 16
    after = (group + 1) % 16

    def greet(i, carry):
        @pl.when(peer(i) != CLERK)
        def _():
            pl.semaphore_signal(barrier, inc=1, device_id={"plane": peer(i)}, device_id_type=MESH)

        return carry

    lax.fori_loop(1, 16, greet, 0)
    for other in (before, after):
        pl.semaphore_signal(
            barrier, inc=1, device_id={"plane": CLERK, "elem": other}, device_id_type=MESH
        )

    def enter_plane():
        @pl.when(me != CLERK)
        def _():
            pl.semaphore_wait(barrier, 15)

        @pl.when(me == LEADER)
        def _():
            pl.semaphore_signal(plane_ok, inc=1, device_id={"plane": CLERK}, device_id_type=MESH)

        @pl.when(me == CLERK)
        def _():
            pl.semaphore_wait(plane_ok, 1)

    def enter_elem():
        @pl.when(me == CLERK)
        def _():
            pl.semaphore_wait(barrier, 32)

            def tell(i, carry):
                pl.semaphore_signal(
                    elem_ok, inc=1, device_id={"plane": peer(i)}, device_id_type=MESH
                )
                return carry

            lax.fori_loop(1, 16, tell, 0)

        @pl.when(me != CLERK)
        def _():
            pl.semaphore_wait(elem_ok, 1)

    def pair_cols(q):
        return pl.ds(pl.multiple_of(128 * q, 128), 128)

    def mode_load(q):
        return pltpu.make_async_copy(modes_hbm.at[:, :, :, pair_cols(q)], modes.at[q], mode_sem.at[q])

    loads = [
        pltpu.make_async_copy(source, target, load_sem.at[i])
        for i, (source, target) in enumerate((
            (pair_hbm, pair),
            (geometry_hbm, geometry),
            (neighbour_hbm, neighbour),
            (neighbour_edge_hbm, neighbour_edge),
            (flipped_hbm, flipped),
            (dense_hbm, dense),
            (wave_hbm, wave),
            (back_wave_hbm, back_wave),
        ))
    ]
    loads[0].start()
    mode_load(peer(2) // 2).start()
    loads[1].start()

    def mode_start(h, carry):
        mode_load(peer(2 * h) // 2).start()
        return carry

    lax.fori_loop(2, 8, mode_start, 0)
    mode_load(z).start()
    for load in loads[2:]:
        load.start()

    def pack(q):
        mode_load(q).wait()
        block = jnp.concatenate([modes[q, c, f] for f in range(3) for c in range(2)], axis=0)
        high, low = split(block)
        send_vel[q] = mm(pair[...], high, NT) + mm(pair[...], low, NT)

    def vel_part(p):
        return send_vel.at[p // 2, pl.ds(pl.multiple_of(p % 2 * 64, 64), 64)]

    def vel_copy(p, slot):
        return pltpu.make_async_remote_copy(
            vel_part(p), recv_vel.at[slot], vel_s.at[p], vel_r.at[slot],
            device_id={"plane": p}, device_id_type=MESH,
        )

    loads[0].wait()
    pack(peer(2) // 2)
    enter_plane()
    vel_copy(peer(2), me).start()
    vel_copy(peer(3), me).start()

    def pack_step(h, carry):
        pack(peer(2 * h) // 2)
        vel_copy(peer(2 * h), me).start()
        vel_copy(peer(2 * h + 1), me).start()
        return carry

    lax.fori_loop(2, 8, pack_step, 0)
    pack(z)
    vel_copy(peer(1), me).start()
    recv_vel[me] = send_vel[z, pl.ds(pl.multiple_of(x * 64, 64), 64), :]

    for load in loads[1:6]:
        load.wait()

    def iota(shape, axis):
        return lax.broadcasted_iota(jnp.int32, shape, axis)

    def rows_of(shape):
        row = iota(shape, 0)
        element = (row * 2731) >> 16
        edge = ((row - element * 24) * 10923) >> 16
        return element, edge, row - element * 24 - edge * 6

    owner = (rows_of((384, 16))[0] == iota((384, 16), 1)).astype(jnp.float32)
    edge = (rows_of((384, 4))[1] == iota((384, 4), 1)).astype(jnp.float32)

    def per_row(table):
        return jnp.sum(exact(owner, table, NT) * edge, axis=1, keepdims=True)

    def one_hot(width, target):
        return iota((384, width), 1).astype(jnp.float32) == target

    near = jnp.maximum(neighbour[...], 0)
    offset = ((near >> 4) - group + 16) & 15
    where = jnp.where(offset == 0, 0, jnp.where(offset == 1, 2, 1))
    start = where * 384 + (near & 15) * 24 + neighbour_edge[...] * 6
    start = per_row(jnp.where(neighbour[...] >= 0, start, -5000).astype(jnp.float32))
    place = rows_of((384, 1))[2].astype(jnp.float32)
    turned = per_row(flipped[...].astype(jnp.float32))
    turned = place + turned * (5.0 - 2.0 * place)
    row = iota((384, 1), 0).astype(jnp.float32)
    turn = jnp.where(one_hot(384, row - place + turned), 1.0, 0.0).astype(jnp.bfloat16)

    for e in range(16):
        left_far[24 * e : 24 * e + 24] = send_vel[e // 2, 64 * (e % 2) : 64 * (e % 2) + 24, :256]
    high, low = split(left_far[...])
    traces[:384] = mm(turn, high) + mm(turn, low)

    enter_elem()

    def swap(array, width, send_sem, recv_sem):
        copies = [
            pltpu.make_async_remote_copy(
                array.at[pl.ds(0, 384)], array.at[pl.ds(384 * (slot + 1), 384)],
                send_sem.at[slot], recv_sem.at[slot],
                device_id={"elem": other}, device_id_type=MESH,
            )
            for slot, other in ((0, after), (1, before))
        ]
        for copy in copies:
            copy.start()
        return copies

    trace_copies = swap(traces, 256, trace_send, trace_recv)
    pick = jnp.where(one_hot(1152, start + place), 1.0, 0.0).astype(jnp.bfloat16)

    geo_column[...] = exact(pair[...].astype(jnp.float32), geometry[:, pair_cols(z)], NT)
    geo = geo_column[pl.ds(pl.multiple_of(64 * x, 64), 64), :]
    joined = jnp.where(neighbour[...] >= 0, 0.5, 0.0)
    edge_own = rows_of((64, 4))[1] + 4 * rows_of((64, 4))[0] == iota((64, 4), 1)
    joined = exact(edge_own.astype(jnp.float32), joined)
    joined = jnp.where(iota((64, 16), 1) == me, joined, 0.0)
    keep = 1.0 - jnp.sum(joined, axis=1, keepdims=True)
    own_xi, own_eta = dense[:64, :64], dense[64:128, :64]
    to_x = geo[:, 0:1] * own_xi + geo[:, 1:2] * own_eta
    to_y = geo[:, 2:3] * own_xi + geo[:, 3:4] * own_eta
    gradient = split(jnp.concatenate([to_x, to_y], axis=0))

    for copy in trace_copies:
        copy.wait_recv()
    high, low = split(traces[...])
    far[...] = mm(pick, high) + mm(pick, low)

    def far_part(p):
        return far.at[pl.ds(pl.multiple_of(24 * p, 8), 24)]

    def far_copy(p, slot):
        return pltpu.make_async_remote_copy(
            far_part(p), recv_far.at[slot], far_s.at[p], far_r.at[slot],
            device_id={"plane": p}, device_id_type=MESH,
        )

    def loop(low, high, body):
        def step(i, carry):
            body(i)
            return carry

        lax.fori_loop(low, high, step, 0)

    loop(2, 12, lambda i: vel_copy(peer(i), me).wait_send())
    loop(2, 4, lambda i: far_copy(peer(i), me).start())
    loop(12, 16, lambda i: vel_copy(peer(i), me).wait_send())
    loop(4, 16, lambda i: far_copy(peer(i), me).start())
    far_copy(peer(1), me).start()
    recv_far[me] = far[pl.ds(pl.multiple_of(24 * me, 8), 24), :]

    for load in loads[6:]:
        load.wait()

    for step, (dz, sources) in enumerate(ARRIVALS):
        for i in sources:
            vel_copy(peer(i), peer(i)).wait_recv()
        part = (z + dz) % 4

        for side in range(2):
            lanes = slice(128 * side, 128 * side + 128)
            a = 2 * part + side
            for f in range(3):
                one = recv_vel[a, :, 128 * f : 128 * f + 128]
                two = recv_vel[a + 8, :, 128 * f : 128 * f + 128]
                one_z = pltpu.roll(one, 64, 1) * dense[pl.ds(128 + a, 1), :]
                two_z = pltpu.roll(two, 64, 1) * dense[pl.ds(136 + a, 1), :]
                for r, (p, q) in enumerate(((one, two), (one_z, two_z))):
                    rows = slice(192 * r + 64 * f, 192 * r + 64 * f + 64)
                    high, low = split(p + q)
                    left_high[0, rows, lanes] = high
                    left_low[0, rows, lanes] = low
                    high, low = split(p - q)
                    left_high[1, rows, lanes] = high
                    left_low[1, rows, lanes] = low

        def inverse(n, first=step == 0, part=part):
            rows = pl.ds(pl.multiple_of(256 * part, 256), 256)
            waves = (wave[0, n, rows, :], wave[1, n, rows, :])
            term = mm3((left_high[n // 2], left_low[n // 2]), waves)
            physical[n] = term if first else physical[n] + term

        loop(0, 4, inverse)

    total[...] = jnp.zeros_like(total)
    total_far[...] = jnp.zeros_like(total_far)

    def advect(n):
        u, v, w = (physical[n, 64 * f : 64 * f + 64] for f in range(3))
        for f, field in enumerate((u, v, w)):
            slopes = mm3(gradient, split(field))
            slopes_edge[n, 24 * f : 24 * f + 24] = slopes[:24]
            slopes_edge[n, 72 + 24 * f : 96 + 24 * f] = slopes[64:88]
            spanwise = physical[n, 192 + 64 * f : 256 + 64 * f]
            product[64 * f : 64 * f + 64] = (
                keep * (u * slopes[:64] + v * slopes[64:]) + w * spanwise
            )
        total[n // 2] += mm3(split(product[...]), (back_wave[0, n], back_wave[1, n]))

    loop(0, 4, advect)

    def both(sums, rows, a):
        lanes = slice(128 * a, 128 * a + 128)
        even, odd = sums[0, rows, lanes], sums[1, rows, lanes]
        return (even + odd) * (1.0 / PLANES), (even - odd) * (1.0 / PLANES)

    def main_copy(part, p, slot):
        rows = pl.ds(*((0, FIRST), (FIRST, 192 - FIRST))[part])
        return pltpu.make_async_remote_copy(
            send_main.at[p, rows], recv_main.at[slot, rows],
            main_s.at[part, p], main_r.at[part, slot],
            device_id={"plane": p}, device_id_type=MESH,
        )

    def send_part(part):
        rows = slice(*((0, FIRST), (FIRST, 192))[part])
        for a in range(8):
            send_main[a, rows], send_main[a + 8, rows] = both(total, rows, a)
        loop(1, 16, lambda i: main_copy(part, peer(i), me).start())
        recv_main[me, rows] = send_main[me, rows]

    send_part(0)

    for step, (dz, sources) in enumerate(ARRIVALS):
        for i in sources:
            far_copy(peer(i), peer(i)).wait_recv()
        part = (z + dz) % 4
        for side in range(2):
            lanes = slice(128 * side, 128 * side + 128)
            a = 2 * part + side
            for f in range(2):
                one = recv_far[a, :, 128 * f : 128 * f + 128]
                two = recv_far[a + 8, :, 128 * f : 128 * f + 128]
                rows = slice(24 * f, 24 * f + 24)
                far_modes[0, rows, lanes] = one + two
                far_modes[1, rows, lanes] = one - two

        def inverse_far(n, first=step == 0, part=part):
            rows = pl.ds(pl.multiple_of(256 * part, 256), 256)
            waves = (wave[0, n, rows, :], wave[1, n, rows, :])
            term = mm3(split(far_modes[n // 2]), waves)
            far_physical[n] = term if first else far_physical[n] + term

        loop(0, 4, inverse_far)

    def advect_far(n):
        u, v = far_physical[n, :24], far_physical[n, 24:]
        terms = jnp.concatenate(
            [
                u * slopes_edge[n, 24 * f : 24 * f + 24]
                + v * slopes_edge[n, 72 + 24 * f : 96 + 24 * f]
                for f in range(3)
            ],
            axis=0,
        )
        total_far[n // 2] += mm3(split(terms), (back_wave[0, n], back_wave[1, n]))

    loop(0, 4, advect_far)

    def back_copy(p, slot):
        return pltpu.make_async_remote_copy(
            send_far.at[p], shares.at[pl.ds(pl.multiple_of(24 * slot, 8), 24)],
            back_s.at[p], back_r.at[slot],
            device_id={"plane": p}, device_id_type=MESH,
        )

    for a in range(8):
        for f in range(3):
            lanes = slice(128 * f, 128 * f + 128)
            plus, minus = both(total_far, slice(24 * f, 24 * f + 24), a)
            send_far[a, :, lanes] = plus
            send_far[a + 8, :, lanes] = minus
    loop(1, 16, lambda i: back_copy(peer(i), me).start())
    shares[pl.ds(pl.multiple_of(24 * me, 8), 24), :] = send_far[me]

    loop(2, MIDDLE, lambda i: back_copy(peer(i), me).wait_send())
    send_part(1)

    loop(1, 16, lambda i: back_copy(peer(i), peer(i)).wait_recv())
    share_copies = swap(shares, 384, share_send, share_recv)
    give = jnp.where(one_hot(1152, start + turned), 0.5, 0.0).astype(jnp.bfloat16)

    for copy in share_copies:
        copy.wait_recv()
    high, low = split(shares[...])
    added[...] = mm(give, high) + mm(give, low)

    def out_copy(q):
        return pltpu.make_async_copy(out.at[q], out_hbm.at[:, :, :, pair_cols(q)], out_sem.at[q])

    def unpack(q):
        rows = pl.ds(pl.multiple_of(48 * q, 16), 48)
        for f in range(3):
            extra = added[rows, 128 * f : 128 * f + 128]
            sides = []
            for side in range(2):
                one = recv_main[2 * q + side, 64 * f : 64 * f + 64]
                sides += [one[:24] + extra[24 * side : 24 * side + 24], one[24:]]
            high, low = split(jnp.concatenate(sides, axis=0))
            block = mm(high, pair[...], TN) + mm(low, pair[...], TN)
            out[q, 0, f] = block[:64]
            out[q, 1, f] = block[64:]
        out_copy(q).start()

    def arrive(i):
        for part in range(2):
            main_copy(part, peer(i), peer(i)).wait_recv()

    def unpack_step(h):
        arrive(2 * h)
        arrive(2 * h + 1)
        unpack(peer(2 * h) // 2)

    arrive(1)
    unpack(z)
    loop(1, 8, unpack_step)

    def drain(i):
        far_copy(peer(i), me).wait_send()
        for part in range(2):
            main_copy(part, peer(i), me).wait_send()

    loop(1, 16, drain)
    vel_copy(peer(1), me).wait_send()
    back_copy(peer(1), me).wait_send()
    loop(EARLY, 16, lambda i: vel_copy(peer(i), me).wait_send())
    loop(MIDDLE, 16, lambda i: back_copy(peer(i), me).wait_send())
    for copy in trace_copies + share_copies:
        copy.wait_send()
    for q in range(8):
        out_copy(q).wait()


def shards(velocity_modes, geometry, neighbour, neighbour_edge, flipped):
    constants = [jnp.asarray(value) for value in tables()]
    anywhere = pl.BlockSpec(memory_space=pl.ANY)
    f32 = jnp.float32
    operands = (velocity_modes, geometry, neighbour.T, neighbour_edge.T, flipped.T, *constants)
    return pl.pallas_call(
        kernel,
        out_shape=jax.ShapeDtypeStruct(velocity_modes.shape, f32),
        in_specs=[anywhere] * len(operands),
        out_specs=anywhere,
        scratch_shapes=[
            pltpu.VMEM((8, 2, 3, 64, 128), f32),
        ]
        + [pltpu.VMEM(value.shape, value.dtype) for value in operands[1:]]
        + [
            pltpu.VMEM((8, 2, 3, 64, 128), f32),
            pltpu.VMEM((128, 4), f32),
            pltpu.VMEM((8, 128, 384), f32),
            pltpu.VMEM((16, 64, 384), f32),
            pltpu.VMEM((1152, 256), f32),
            pltpu.VMEM((384, 256), f32),
            pltpu.VMEM((16, 24, 256), f32),
            pltpu.VMEM((2, 384, 256), jnp.bfloat16),
            pltpu.VMEM((2, 384, 256), jnp.bfloat16),
            pltpu.VMEM((4, 384, 256), f32),
            pltpu.VMEM((384, 256), f32),
            pltpu.VMEM((2, 48, 256), f32),
            pltpu.VMEM((4, 48, 256), f32),
            pltpu.VMEM((4, 144, 256), f32),
            pltpu.VMEM((192, 256), f32),
            pltpu.VMEM((2, 192, 1024), f32),
            pltpu.VMEM((2, 72, 1024), f32),
            pltpu.VMEM((16, 192, 128), f32),
            pltpu.VMEM((16, 192, 128), f32),
            pltpu.VMEM((16, 24, 384), f32),
            pltpu.VMEM((1152, 384), f32),
            pltpu.VMEM((384, 384), f32),
            pltpu.SemaphoreType.REGULAR,
            pltpu.SemaphoreType.REGULAR,
            pltpu.SemaphoreType.DMA((9,)),
            pltpu.SemaphoreType.DMA((8,)),
            pltpu.SemaphoreType.DMA((8,)),
        ]
        + [pltpu.SemaphoreType.DMA((2,))] * 4
        + [pltpu.SemaphoreType.DMA((16,))] * 4
        + [pltpu.SemaphoreType.DMA((2, 16))] * 2
        + [pltpu.SemaphoreType.DMA((16,))] * 2,
        compiler_params=pltpu.CompilerParams(
            collective_id=0, has_side_effects=True, vmem_limit_bytes=56 * 2**20
        ),
    )(*operands)


def solution(mesh):
    placed = (
        P(None, None, "plane", "elem"),
        P(None, "elem"),
        P("elem", None),
        P("elem", None),
        P("elem", None),
    )
    return jax.shard_map(
        shards,
        mesh=mesh,
        in_specs=placed,
        out_specs=P(None, None, "plane", "elem"),
        check_vma=False,
    )
```

```python
import jax
import jax.numpy as jnp
import ml_dtypes
import numpy as np
from jax import lax
from jax.experimental import pallas as pl
from jax.experimental.pallas import tpu as pltpu
from jax.sharding import PartitionSpec as P

PLANES = 1024
POINTS = 64
LEADER, CLERK = 0, 1
EARLY, MIDDLE = 16, 12
ARRIVALS = ((1, (2, 3, 12, 13)), (3, (4, 5, 10, 11)), (2, (6, 7, 8, 9)), (0, (14, 15, 1)))
FIRST = 64
MESH = pl.DeviceIdType.MESH
highest = lax.Precision.HIGHEST
gll_nodes = [
    -1.0,
    -0.8717401485096066,
    -0.5917001814331423,
    -0.2092992179024789,
    0.2092992179024789,
    0.5917001814331423,
    0.8717401485096066,
    1.0,
]


def legendre_seven(point_value):
    earlier_value = 1.0
    current_value = point_value
    for degree_index in range(1, 7):
        next_value = (
            (2 * degree_index + 1) * point_value * current_value - degree_index * earlier_value
        ) / (degree_index + 1)
        earlier_value = current_value
        current_value = next_value
    return current_value


def gll_matrices():
    legendre_vals = [legendre_seven(node_value) for node_value in gll_nodes]
    deriv_matrix = np.zeros((8, 8))
    for row_index in range(8):
        for col_index in range(8):
            if row_index != col_index:
                deriv_matrix[row_index, col_index] = (
                    legendre_vals[row_index]
                    / legendre_vals[col_index]
                    / (gll_nodes[row_index] - gll_nodes[col_index])
                )
    deriv_matrix[0, 0] = -14.0
    deriv_matrix[7, 7] = 14.0
    identity = np.eye(8)
    return (np.kron(identity, deriv_matrix), np.kron(deriv_matrix, identity))


def halves(matrix):
    high = matrix.astype(ml_dtypes.bfloat16)
    low = (matrix - high.astype(np.float64)).astype(ml_dtypes.bfloat16)
    return high, low


def point_order():
    steps = range(1, 7)
    order = [p for p in steps] + [8 * p + 7 for p in steps]
    order += [56 + p for p in steps] + [8 * p for p in steps]
    return order + [r for r in range(POINTS) if r not in order]


def tables():
    order = point_order()
    xi, eta = gll_matrices()
    pair = np.kron(np.eye(2), np.eye(POINTS)[order]).astype(ml_dtypes.bfloat16)

    k = (64 * np.arange(8)[:, None] + np.arange(64)[None, :])[:, None, :]
    waves = []
    for block in range(4):
        plane = 2 * (256 * (block % 2) + np.arange(256)) + block // 2
        angle = (k[..., None] * plane) % PLANES * (2.0 * np.pi / PLANES)
        waves.append(np.concatenate([np.cos(angle), -np.sin(angle)], axis=1).reshape(1024, 256))
    wave = np.stack(halves(np.stack(waves)))

    mode = 64 * np.arange(16)[:, None] + np.arange(64)[None, :]
    factor = 2.0 * np.where(mode < 512, mode, mode - 1024)
    dense = np.zeros((144, 128), np.float32)
    dense[:64, :64] = xi[order][:, order]
    dense[64:128, :64] = eta[order][:, order]
    dense[128:] = np.concatenate([-factor, factor], axis=1)
    return pair, dense, wave, np.ascontiguousarray(wave.transpose(0, 1, 3, 2))


def split(x):
    high = x.astype(jnp.bfloat16)
    return high, (x - high.astype(jnp.float32)).astype(jnp.bfloat16)


def mm(a, b, dims=((1,), (0,))):
    return lax.dot_general(a, b, (dims, ((), ())), preferred_element_type=jnp.float32)


NT = ((1,), (1,))
TN = ((0,), (0,))


def mm3(a, b, dims=((1,), (0,))):
    return mm(a[0], b[0], dims) + (mm(a[0], b[1], dims) + mm(a[1], b[0], dims))


def exact(a, b, dims=((1,), (0,))):
    return lax.dot_general(
        a, b, (dims, ((), ())), precision=highest, preferred_element_type=jnp.float32
    )


def kernel(
    modes_hbm, geometry_hbm, neighbour_hbm, neighbour_edge_hbm, flipped_hbm,
    pair_hbm, dense_hbm, wave_hbm, back_wave_hbm,
    out_hbm,
    modes, geometry, neighbour, neighbour_edge, flipped, pair, dense, wave, back_wave, out,
    geo_column, send_vel, recv_vel, traces, far, recv_far, left_high, left_low, physical,
    left_far, far_modes, far_physical, slopes_edge, product, total, total_far, send_main, recv_main, send_far, shares, added,
    plane_ok, elem_ok, load_sem, mode_sem, out_sem,
    trace_send, trace_recv, share_send, share_recv, vel_s, vel_r, far_s, far_r, main_s, main_r, back_s, back_r,
):
    me = lax.axis_index("plane")
    group = lax.axis_index("elem")
    z = me // 2
    x = me % 2

    def peer(i):
        h = i // 2
        dz = (h + 1) // 2 * (2 * (h % 2) - 1)
        return (z + dz + 8) % 8 * 2 + (x + i) % 2

    barrier = pltpu.get_barrier_semaphore()
    before = (group + 15) % 16
    after = (group + 1) % 16

    def greet(i, carry):
        @pl.when(peer(i) != CLERK)
        def _():
            pl.semaphore_signal(barrier, inc=1, device_id={"plane": peer(i)}, device_id_type=MESH)

        return carry

    lax.fori_loop(1, 16, greet, 0)
    for other in (before, after):
        pl.semaphore_signal(
            barrier, inc=1, device_id={"plane": CLERK, "elem": other}, device_id_type=MESH
        )

    def enter_plane():
        @pl.when(me != CLERK)
        def _():
            pl.semaphore_wait(barrier, 15)

        @pl.when(me == LEADER)
        def _():
            pl.semaphore_signal(plane_ok, inc=1, device_id={"plane": CLERK}, device_id_type=MESH)

        @pl.when(me == CLERK)
        def _():
            pl.semaphore_wait(plane_ok, 1)

    def enter_elem():
        @pl.when(me == CLERK)
        def _():
            pl.semaphore_wait(barrier, 32)

            def tell(i, carry):
                pl.semaphore_signal(
                    elem_ok, inc=1, device_id={"plane": peer(i)}, device_id_type=MESH
                )
                return carry

            lax.fori_loop(1, 16, tell, 0)

        @pl.when(me != CLERK)
        def _():
            pl.semaphore_wait(elem_ok, 1)

    def pair_cols(q):
        return pl.ds(pl.multiple_of(128 * q, 128), 128)

    def mode_load(q):
        return pltpu.make_async_copy(modes_hbm.at[:, :, :, pair_cols(q)], modes.at[q], mode_sem.at[q])

    loads = [
        pltpu.make_async_copy(source, target, load_sem.at[i])
        for i, (source, target) in enumerate((
            (pair_hbm, pair),
            (geometry_hbm, geometry),
            (neighbour_hbm, neighbour),
            (neighbour_edge_hbm, neighbour_edge),
            (flipped_hbm, flipped),
            (dense_hbm, dense),
            (wave_hbm, wave),
            (back_wave_hbm, back_wave),
        ))
    ]
    loads[0].start()
    mode_load(peer(2) // 2).start()
    loads[1].start()

    def mode_start(h, carry):
        mode_load(peer(2 * h) // 2).start()
        return carry

    lax.fori_loop(2, 8, mode_start, 0)
    mode_load(z).start()
    for load in loads[2:]:
        load.start()

    def pack(q):
        mode_load(q).wait()
        block = jnp.concatenate([modes[q, c, f] for f in range(3) for c in range(2)], axis=0)
        high, low = split(block)
        send_vel[q] = mm(pair[...], high, NT) + mm(pair[...], low, NT)

    def vel_part(p):
        return send_vel.at[p // 2, pl.ds(pl.multiple_of(p % 2 * 64, 64), 64)]

    def vel_copy(p, slot):
        return pltpu.make_async_remote_copy(
            vel_part(p), recv_vel.at[slot], vel_s.at[p], vel_r.at[slot],
            device_id={"plane": p}, device_id_type=MESH,
        )

    loads[0].wait()
    pack(peer(2) // 2)
    enter_plane()
    vel_copy(peer(2), me).start()
    vel_copy(peer(3), me).start()

    def pack_step(h, carry):
        pack(peer(2 * h) // 2)
        vel_copy(peer(2 * h), me).start()
        vel_copy(peer(2 * h + 1), me).start()
        return carry

    lax.fori_loop(2, 8, pack_step, 0)
    pack(z)
    vel_copy(peer(1), me).start()
    recv_vel[me] = send_vel[z, pl.ds(pl.multiple_of(x * 64, 64), 64), :]

    for load in loads[1:6]:
        load.wait()

    def iota(shape, axis):
        return lax.broadcasted_iota(jnp.int32, shape, axis)

    def rows_of(shape):
        row = iota(shape, 0)
        element = (row * 2731) >> 16
        edge = ((row - element * 24) * 10923) >> 16
        return element, edge, row - element * 24 - edge * 6

    owner = (rows_of((384, 16))[0] == iota((384, 16), 1)).astype(jnp.float32)
    edge = (rows_of((384, 4))[1] == iota((384, 4), 1)).astype(jnp.float32)

    def per_row(table):
        return jnp.sum(exact(owner, table, NT) * edge, axis=1, keepdims=True)

    def one_hot(width, target):
        return iota((384, width), 1).astype(jnp.float32) == target

    near = jnp.maximum(neighbour[...], 0)
    offset = ((near >> 4) - group + 16) & 15
    where = jnp.where(offset == 0, 0, jnp.where(offset == 1, 2, 1))
    start = where * 384 + (near & 15) * 24 + neighbour_edge[...] * 6
    start = per_row(jnp.where(neighbour[...] >= 0, start, -5000).astype(jnp.float32))
    place = rows_of((384, 1))[2].astype(jnp.float32)
    turned = per_row(flipped[...].astype(jnp.float32))
    turned = place + turned * (5.0 - 2.0 * place)
    row = iota((384, 1), 0).astype(jnp.float32)
    turn = jnp.where(one_hot(384, row - place + turned), 1.0, 0.0).astype(jnp.bfloat16)

    for e in range(16):
        left_far[24 * e : 24 * e + 24] = send_vel[e // 2, 64 * (e % 2) : 64 * (e % 2) + 24, :256]
    high, low = split(left_far[...])
    traces[:384] = mm(turn, high) + mm(turn, low)

    enter_elem()

    def swap(array, width, send_sem, recv_sem):
        copies = [
            pltpu.make_async_remote_copy(
                array.at[pl.ds(0, 384)], array.at[pl.ds(384 * (slot + 1), 384)],
                send_sem.at[slot], recv_sem.at[slot],
                device_id={"elem": other}, device_id_type=MESH,
            )
            for slot, other in ((0, after), (1, before))
        ]
        for copy in copies:
            copy.start()
        return copies

    trace_copies = swap(traces, 256, trace_send, trace_recv)
    pick = jnp.where(one_hot(1152, start + place), 1.0, 0.0).astype(jnp.bfloat16)

    geo_column[...] = exact(pair[...].astype(jnp.float32), geometry[:, pair_cols(z)], NT)
    geo = geo_column[pl.ds(pl.multiple_of(64 * x, 64), 64), :]
    joined = jnp.where(neighbour[...] >= 0, 0.5, 0.0)
    edge_own = rows_of((64, 4))[1] + 4 * rows_of((64, 4))[0] == iota((64, 4), 1)
    joined = exact(edge_own.astype(jnp.float32), joined)
    joined = jnp.where(iota((64, 16), 1) == me, joined, 0.0)
    keep = 1.0 - jnp.sum(joined, axis=1, keepdims=True)
    own_xi, own_eta = dense[:64, :64], dense[64:128, :64]
    to_x = geo[:, 0:1] * own_xi + geo[:, 1:2] * own_eta
    to_y = geo[:, 2:3] * own_xi + geo[:, 3:4] * own_eta
    gradient = split(jnp.concatenate([to_x, to_y], axis=0))

    for copy in trace_copies:
        copy.wait_recv()
    high, low = split(traces[...])
    far[...] = mm(pick, high) + mm(pick, low)

    def far_part(p):
        return far.at[pl.ds(pl.multiple_of(24 * p, 8), 24)]

    def far_copy(p, slot):
        return pltpu.make_async_remote_copy(
            far_part(p), recv_far.at[slot], far_s.at[p], far_r.at[slot],
            device_id={"plane": p}, device_id_type=MESH,
        )

    def loop(low, high, body):
        def step(i, carry):
            body(i)
            return carry

        lax.fori_loop(low, high, step, 0)

    loop(2, 12, lambda i: vel_copy(peer(i), me).wait_send())
    loop(2, 4, lambda i: far_copy(peer(i), me).start())
    loop(12, 16, lambda i: vel_copy(peer(i), me).wait_send())
    loop(4, 16, lambda i: far_copy(peer(i), me).start())
    far_copy(peer(1), me).start()
    recv_far[me] = far[pl.ds(pl.multiple_of(24 * me, 8), 24), :]

    for load in loads[6:]:
        load.wait()

    for step, (dz, sources) in enumerate(ARRIVALS):
        for i in sources:
            vel_copy(peer(i), peer(i)).wait_recv()
        part = (z + dz) % 4

        for side in range(2):
            lanes = slice(128 * side, 128 * side + 128)
            a = 2 * part + side
            for f in range(3):
                one = recv_vel[a, :, 128 * f : 128 * f + 128]
                two = recv_vel[a + 8, :, 128 * f : 128 * f + 128]
                one_z = pltpu.roll(one, 64, 1) * dense[pl.ds(128 + a, 1), :]
                two_z = pltpu.roll(two, 64, 1) * dense[pl.ds(136 + a, 1), :]
                for r, (p, q) in enumerate(((one, two), (one_z, two_z))):
                    rows = slice(192 * r + 64 * f, 192 * r + 64 * f + 64)
                    high, low = split(p + q)
                    left_high[0, rows, lanes] = high
                    left_low[0, rows, lanes] = low
                    high, low = split(p - q)
                    left_high[1, rows, lanes] = high
                    left_low[1, rows, lanes] = low

        def inverse(n, first=step == 0, part=part):
            rows = pl.ds(pl.multiple_of(256 * part, 256), 256)
            waves = (wave[0, n, rows, :], wave[1, n, rows, :])
            term = mm3((left_high[n // 2], left_low[n // 2]), waves)
            physical[n] = term if first else physical[n] + term

        loop(0, 4, inverse)

    total[...] = jnp.zeros_like(total)
    total_far[...] = jnp.zeros_like(total_far)

    def advect(n):
        u, v, w = (physical[n, 64 * f : 64 * f + 64] for f in range(3))
        for f, field in enumerate((u, v, w)):
            slopes = mm3(gradient, split(field))
            slopes_edge[n, 24 * f : 24 * f + 24] = slopes[:24]
            slopes_edge[n, 72 + 24 * f : 96 + 24 * f] = slopes[64:88]
            spanwise = physical[n, 192 + 64 * f : 256 + 64 * f]
            product[64 * f : 64 * f + 64] = (
                keep * (u * slopes[:64] + v * slopes[64:]) + w * spanwise
            )
        total[n // 2] += mm3(split(product[...]), (back_wave[0, n], back_wave[1, n]))

    loop(0, 4, advect)

    def both(sums, rows, a):
        lanes = slice(128 * a, 128 * a + 128)
        even, odd = sums[0, rows, lanes], sums[1, rows, lanes]
        return (even + odd) * (1.0 / PLANES), (even - odd) * (1.0 / PLANES)

    def main_copy(part, p, slot):
        rows = pl.ds(*((0, FIRST), (FIRST, 192 - FIRST))[part])
        return pltpu.make_async_remote_copy(
            send_main.at[p, rows], recv_main.at[slot, rows],
            main_s.at[part, p], main_r.at[part, slot],
            device_id={"plane": p}, device_id_type=MESH,
        )

    def send_part(part):
        rows = slice(*((0, FIRST), (FIRST, 192))[part])
        for a in range(8):
            send_main[a, rows], send_main[a + 8, rows] = both(total, rows, a)
        loop(1, 16, lambda i: main_copy(part, peer(i), me).start())
        recv_main[me, rows] = send_main[me, rows]

    send_part(0)

    for step, (dz, sources) in enumerate(ARRIVALS):
        for i in sources:
            far_copy(peer(i), peer(i)).wait_recv()
        part = (z + dz) % 4
        for side in range(2):
            lanes = slice(128 * side, 128 * side + 128)
            a = 2 * part + side
            for f in range(2):
                one = recv_far[a, :, 128 * f : 128 * f + 128]
                two = recv_far[a + 8, :, 128 * f : 128 * f + 128]
                rows = slice(24 * f, 24 * f + 24)
                far_modes[0, rows, lanes] = one + two
                far_modes[1, rows, lanes] = one - two

        def inverse_far(n, first=step == 0, part=part):
            rows = pl.ds(pl.multiple_of(256 * part, 256), 256)
            waves = (wave[0, n, rows, :], wave[1, n, rows, :])
            term = mm3(split(far_modes[n // 2]), waves)
            far_physical[n] = term if first else far_physical[n] + term

        loop(0, 4, inverse_far)

    def advect_far(n):
        u, v = far_physical[n, :24], far_physical[n, 24:]
        terms = jnp.concatenate(
            [
                u * slopes_edge[n, 24 * f : 24 * f + 24]
                + v * slopes_edge[n, 72 + 24 * f : 96 + 24 * f]
                for f in range(3)
            ],
            axis=0,
        )
        total_far[n // 2] += mm3(split(terms), (back_wave[0, n], back_wave[1, n]))

    loop(0, 4, advect_far)

    def back_copy(p, slot):
        return pltpu.make_async_remote_copy(
            send_far.at[p], shares.at[pl.ds(pl.multiple_of(24 * slot, 8), 24)],
            back_s.at[p], back_r.at[slot],
            device_id={"plane": p}, device_id_type=MESH,
        )

    for a in range(8):
        for f in range(3):
            lanes = slice(128 * f, 128 * f + 128)
            plus, minus = both(total_far, slice(24 * f, 24 * f + 24), a)
            send_far[a, :, lanes] = plus
            send_far[a + 8, :, lanes] = minus
    loop(1, 16, lambda i: back_copy(peer(i), me).start())
    shares[pl.ds(pl.multiple_of(24 * me, 8), 24), :] = send_far[me]

    loop(2, MIDDLE, lambda i: back_copy(peer(i), me).wait_send())
    send_part(1)

    loop(1, 16, lambda i: back_copy(peer(i), peer(i)).wait_recv())
    share_copies = swap(shares, 384, share_send, share_recv)
    give = jnp.where(one_hot(1152, start + turned), 0.5, 0.0).astype(jnp.bfloat16)

    for copy in share_copies:
        copy.wait_recv()
    high, low = split(shares[...])
    added[...] = mm(give, high) + mm(give, low)

    def out_copy(q):
        return pltpu.make_async_copy(out.at[q], out_hbm.at[:, :, :, pair_cols(q)], out_sem.at[q])

    def unpack(q):
        rows = pl.ds(pl.multiple_of(48 * q, 16), 48)
        for f in range(3):
            extra = added[rows, 128 * f : 128 * f + 128]
            sides = []
            for side in range(2):
                one = recv_main[2 * q + side, 64 * f : 64 * f + 64]
                sides += [one[:24] + extra[24 * side : 24 * side + 24], one[24:]]
            high, low = split(jnp.concatenate(sides, axis=0))
            block = mm(high, pair[...], TN) + mm(low, pair[...], TN)
            out[q, 0, f] = block[:64]
            out[q, 1, f] = block[64:]
        out_copy(q).start()

    def arrive(i):
        for part in range(2):
            main_copy(part, peer(i), peer(i)).wait_recv()

    def unpack_step(h):
        arrive(2 * h)
        arrive(2 * h + 1)
        unpack(peer(2 * h) // 2)

    arrive(1)
    unpack(z)
    loop(1, 8, unpack_step)

    def drain(i):
        far_copy(peer(i), me).wait_send()
        for part in range(2):
            main_copy(part, peer(i), me).wait_send()

    loop(1, 16, drain)
    vel_copy(peer(1), me).wait_send()
    back_copy(peer(1), me).wait_send()
    loop(EARLY, 16, lambda i: vel_copy(peer(i), me).wait_send())
    loop(MIDDLE, 16, lambda i: back_copy(peer(i), me).wait_send())
    for copy in trace_copies + share_copies:
        copy.wait_send()
    for q in range(8):
        out_copy(q).wait()


def shards(velocity_modes, geometry, neighbour, neighbour_edge, flipped):
    constants = [jnp.asarray(value) for value in tables()]
    anywhere = pl.BlockSpec(memory_space=pl.ANY)
    f32 = jnp.float32
    operands = (velocity_modes, geometry, neighbour.T, neighbour_edge.T, flipped.T, *constants)
    return pl.pallas_call(
        kernel,
        out_shape=jax.ShapeDtypeStruct(velocity_modes.shape, f32),
        in_specs=[anywhere] * len(operands),
        out_specs=anywhere,
        scratch_shapes=[
            pltpu.VMEM((8, 2, 3, 64, 128), f32),
        ]
        + [pltpu.VMEM(value.shape, value.dtype) for value in operands[1:]]
        + [
            pltpu.VMEM((8, 2, 3, 64, 128), f32),
            pltpu.VMEM((128, 4), f32),
            pltpu.VMEM((8, 128, 384), f32),
            pltpu.VMEM((16, 64, 384), f32),
            pltpu.VMEM((1152, 256), f32),
            pltpu.VMEM((384, 256), f32),
            pltpu.VMEM((16, 24, 256), f32),
            pltpu.VMEM((2, 384, 256), jnp.bfloat16),
            pltpu.VMEM((2, 384, 256), jnp.bfloat16),
            pltpu.VMEM((4, 384, 256), f32),
            pltpu.VMEM((384, 256), f32),
            pltpu.VMEM((2, 48, 256), f32),
            pltpu.VMEM((4, 48, 256), f32),
            pltpu.VMEM((4, 144, 256), f32),
            pltpu.VMEM((192, 256), f32),
            pltpu.VMEM((2, 192, 1024), f32),
            pltpu.VMEM((2, 72, 1024), f32),
            pltpu.VMEM((16, 192, 128), f32),
            pltpu.VMEM((16, 192, 128), f32),
            pltpu.VMEM((16, 24, 384), f32),
            pltpu.VMEM((1152, 384), f32),
            pltpu.VMEM((384, 384), f32),
            pltpu.SemaphoreType.REGULAR,
            pltpu.SemaphoreType.REGULAR,
            pltpu.SemaphoreType.DMA((9,)),
            pltpu.SemaphoreType.DMA((8,)),
            pltpu.SemaphoreType.DMA((8,)),
        ]
        + [pltpu.SemaphoreType.DMA((2,))] * 4
        + [pltpu.SemaphoreType.DMA((16,))] * 4
        + [pltpu.SemaphoreType.DMA((2, 16))] * 2
        + [pltpu.SemaphoreType.DMA((16,))] * 2,
        compiler_params=pltpu.CompilerParams(
            collective_id=0, has_side_effects=True, vmem_limit_bytes=56 * 2**20
        ),
    )(*operands)


def solution(mesh):
    placed = (
        P(None, None, "plane", "elem"),
        P(None, "elem"),
        P("elem", None),
        P("elem", None),
        P("elem", None),
    )
    return jax.shard_map(
        shards,
        mesh=mesh,
        in_specs=placed,
        out_specs=P(None, None, "plane", "elem"),
        check_vma=False,
    )
```
